128 devices in a mesh: ep: 32 (over z, x, core), tp: 4 (over y).
Axes of the slice: x: 4, y: 4, z: 4, core: 2. Of those that a mesh axis runs over, the one named last changes fastest.
Arguments:
- tokens: bfloat16 [12288, 2048], P('ep'), may hold values from -6 to 6
- doc_ids: int32 [12288], P('ep'), may hold values from 0 to 63, never falling along the last dimension, each value on 1 to 384 neighbouring positions
- routes: int32 [12288, 8], P('ep'), may hold values from 0 to 127, all different within a row; in each aligned block of 384 rows (0 to 383, 384 to 767, ...) at most 32 rows name the same one
- query_weight: bfloat16 [2048, 4096], P(None, 'tp'), may hold values from -0.125 to 0.125
- key_matrix: bfloat16 [2048, 512], P(None, 'tp'), may hold values from -0.125 to 0.125
- value_matrix: bfloat16 [2048, 512], P(None, 'tp'), may hold values from -0.125 to 0.125
- output_weight: bfloat16 [2048, 4096], P(None, 'tp'), may hold values from -0.75 to 0.75
- attn_gain: float32 [2048], replicated, may hold values from 0.5 to 1.5
- query_gain: float32 [128], replicated, may hold values from 0.5 to 1.5
- key_gain: float32 [128], replicated, may hold values from 0.5 to 1.5
- mlp_gain: float32 [2048], replicated, may hold values from 0.5 to 1.5
- router_weight: bfloat16 [2048, 128], replicated, may hold values from -0.0625 to 0.0625
- gate_weight: bfloat16 [128, 2048, 768], P('ep', None, 'tp'), may hold values from -0.125 to 0.125
- up_weight: bfloat16 [128, 2048, 768], P('ep', None, 'tp'), may hold values from -0.125 to 0.125
- down_weight: bfloat16 [128, 768, 2048], P('ep', 'tp'), may hold values from -0.625 to 0.625
- cotangent: bfloat16 [12288, 2048], P('ep'), may hold values from -6 to 6
Outputs:
- layer_out: bfloat16 [12288, 2048], P('ep')
- tokens_grad: bfloat16 [12288, 2048], P('ep')
- query_wgrad: float32 [2048, 4096], P('ep', 'tp')
- key_wgrad: float32 [2048, 512], P('ep', 'tp')
- value_wgrad: float32 [2048, 512], P('ep', 'tp')
- output_wgrad: float32 [2048, 4096], P('ep', 'tp')
- attn_gain_grad: float32 [2048], P('ep')
- query_gain_grad: float32 [128], replicated
- key_gain_grad: float32 [128], replicated
- mlp_gain_grad: float32 [2048], P('ep')
- router_wgrad: float32 [2048, 128], P('ep')
- gate_wgrad: float32 [128, 2048, 768], P('ep', None, 'tp')
- up_wgrad: float32 [128, 2048, 768], P('ep', None, 'tp')
- down_wgrad: float32 [128, 768, 2048], P('ep', 'tp')
The draws below stay inside these ranges and needn't reach their ends.
Inputs may be any that keep to these rules, and one draw needn't show every extreme that they name: `routes`: in the rows of one device (aligned blocks of 384 rows) no expert is named by more than 32 rows, a bound that some block reaches. A row names 8 different experts. `doc_ids`: document numbers never fall along the whole array; a document holds 1 to 384 tokens and one holds exactly 384.
All inputs are finite; a program needn't handle non-finite values.
Results may differ from the reference program's by a relative error of at most 0.03.
Values may be sent and summed in bfloat16 or wider, within the bound.
No kernel may reach another device: no remote copies, remote signals or barrier semaphores. Data moves between devices by JAX's collectives and lax.ppermute only.
A program may use at most 448 MiB of HBM per device.

```python
import math
import jax
import jax.numpy as jnp
import numpy as np
from jax import lax

MODEL_WIDTH = 2048
QUERY_HEAD_COUNT = 32
KEY_VALUE_HEADS = 4
HEAD_SIZE = 128
FF = 768
TOP = 8
SEQUENCE_LENGTH = 384
EXPERTS = 128
TOKENS = 12288
CAP = 32
N_EP = 32


def block_levels(stream_key, extent, shards, least, high):
    def one(position, shards_of):
        steps = jax.random.uniform(jax.random.fold_in(jax.random.fold_in(stream_key, 6), position), (shards_of,), jnp.float32, least / len(shards), high / len(shards))
        return jnp.repeat(jnp.exp(steps), extent[position] // shards_of).reshape((-1,) + (1,) * (len(extent) - position - 1))

    level = one(*shards[0])
    for cut in shards[1:]:
        level = level * one(*cut)
    return level


def length_profile(amount, total, most, skew):
    weights = [(1 << 20) // math.isqrt(standing ** skew) + 1 for standing in range(2, amount + 1)]
    rest, given = total - most - (amount - 1), [1] * (amount - 1)
    while rest > 0:
        free = [i for i in range(amount - 1) if given[i] < most]
        whole, remaining = sum([weights[i] for i in free]), rest
        for i in free:
            addition = min(most - given[i], max(1, remaining * weights[i] // whole), rest)
            given[i] = given[i] + addition
            rest = rest - addition
    return np.array([most] + given)


def uneven_parts(rng, amount, total, limit, slope):
    if amount == 2:
        one = jax.random.randint(rng, (), max(1, total - limit), min(limit, total - 1) + 1)
        return jnp.stack([one, total - one])
    lengths = jnp.asarray(length_profile(amount, total, limit, slope), jnp.int32)
    pairs = (amount - 1) // 2
    source_of, receiver = lengths[1:1 + 2 * pairs:2], lengths[2:2 + 2 * pairs:2]
    margin = jnp.minimum(source_of - 1, limit - receiver)
    moved = jax.random.randint(jax.random.fold_in(rng, 1), (pairs,), 0, 1 << 20) % (margin + 1)
    lengths = lengths.at[1:1 + 2 * pairs:2].set(source_of - moved).at[2:2 + 2 * pairs:2].set(receiver + moved)
    return lengths[jax.random.permutation(jax.random.fold_in(rng, 2), amount)]


def deal_out(own_key, own, number, rows, amount, top, reach, slope):
    order = jax.random.permutation(own_key, amount)
    crowded, usual = load_shares(amount, rows * top, reach, slope, True), load_shares(amount, rows * top, reach, slope, False)
    places = jnp.arange(amount)

    def named(lengths, turn):
        used = int((lengths > 0).sum())
        fixed = max(1, used // 4)
        moved = fixed + (places - fixed + turn * (used - fixed)) % max(1, amount - fixed)
        return jnp.zeros((amount,), jnp.int32).at[order[jnp.where(places < fixed, places, moved)]].set(jnp.asarray(lengths, jnp.int32))

    lengths = jnp.where(number % 4 == 0, named(crowded, number // 4), named(usual, number - number // 4 - 1))
    mixed = jax.random.permutation(jax.random.fold_in(own, 3), amount)
    source_of, sink = mixed[0:amount // 2 * 2:2], mixed[1:amount // 2 * 2:2]
    slack = jnp.minimum(lengths[source_of] - 1, reach - lengths[sink]) // 2
    slack = jnp.where((source_of == order[0]) | (sink == order[0]) | (lengths[sink] == 0), 0, jnp.maximum(slack, 0))
    moved = jax.random.randint(jax.random.fold_in(own, 4), (amount // 2,), 0, 1 << 20) % (slack + 1)
    lengths = lengths.at[source_of].add(-moved).at[sink].add(moved)
    items = jnp.searchsorted(jnp.cumsum(lengths), jnp.arange(rows * top), side="right").astype(jnp.int32)
    grid = items.reshape(top, rows).T
    grid = grid[jax.random.permutation(jax.random.fold_in(own, 1), rows)]
    turn = jax.random.randint(jax.random.fold_in(own, 2), (rows, 1), 0, top)
    return jnp.take_along_axis(grid, (jnp.arange(top)[None, :] + turn) % top, axis=1)


def load_shares(amount, total, reach, slope, full):
    loads = [(1 << 20) // math.isqrt(grade ** slope) + 1 for grade in range(1, amount + 1)]
    largest = reach if full else min(reach, max(-(-total // amount), total * loads[0] // sum(loads)))
    least = 1 if total - largest >= amount - 1 else 0
    given, spare = [largest] + [least] * (amount - 1), total - largest - least * (amount - 1)
    while spare > 0:
        movable = [i for i in range(1, amount) if given[i] < largest] or [i for i in range(1, amount) if given[i] < reach]
        whole, budget = sum([loads[i] for i in movable]), spare
        for i in movable:
            more = min(reach - given[i], max(1, budget * loads[i] // whole), spare)
            given[i] = given[i] + more
            spare = spare - more
    return np.array(given)


def scatter_about(own_key, shape, spread, reach, pieces=(), kind=jnp.bfloat16):
    drawn = spread * jax.random.normal(own_key, shape, jnp.float32)
    if pieces:
        drawn = drawn * block_levels(own_key, shape, pieces, -0.22, 0.18)
    return jnp.clip(drawn, -reach, reach).astype(kind)


def setup_inputs(seed: int = 0) -> dict:
    arg_keys = jax.random.split(jax.random.key(seed), 17)
    tokens = scatter_about(arg_keys[0], (TOKENS, MODEL_WIDTH), 1.0, 6.0, ((0, 32),))
    doc_ids = jnp.searchsorted(jnp.cumsum(uneven_parts(arg_keys[1], 2 * TOKENS // SEQUENCE_LENGTH, TOKENS, SEQUENCE_LENGTH, 2)), jnp.arange(TOKENS), side="right").astype(jnp.int32)
    routes_keys = jax.random.split(jax.random.fold_in(arg_keys[2], 1), TOKENS // SEQUENCE_LENGTH)
    routes_turns = jax.random.permutation(jax.random.fold_in(arg_keys[2], 3), TOKENS // SEQUENCE_LENGTH)
    routes = jax.vmap(lambda own, number: deal_out(jax.random.fold_in(arg_keys[2], 2), own, number, SEQUENCE_LENGTH, EXPERTS, TOP, CAP, 1))(routes_keys, routes_turns).reshape((TOKENS, TOP))
    query_weight = scatter_about(arg_keys[3], (MODEL_WIDTH, QUERY_HEAD_COUNT * HEAD_SIZE), MODEL_WIDTH ** -0.5, 0.125, ((1, 4),))
    key_matrix = scatter_about(arg_keys[4], (MODEL_WIDTH, KEY_VALUE_HEADS * HEAD_SIZE), MODEL_WIDTH ** -0.5, 0.125, ((1, 4),))
    value_matrix = scatter_about(arg_keys[5], (MODEL_WIDTH, KEY_VALUE_HEADS * HEAD_SIZE), MODEL_WIDTH ** -0.5, 0.125, ((1, 4),))
    output_weight = scatter_about(arg_keys[6], (MODEL_WIDTH, QUERY_HEAD_COUNT * HEAD_SIZE), (QUERY_HEAD_COUNT * HEAD_SIZE // 64) ** -0.5, 0.75, ((1, 4),))
    attn_gain = jnp.clip(1.0 + 0.1 * jax.random.normal(arg_keys[7], (MODEL_WIDTH,), jnp.float32), 0.5, 1.5)
    query_gain = jnp.clip(1.0 + 0.1 * jax.random.normal(arg_keys[8], (HEAD_SIZE,), jnp.float32), 0.5, 1.5)
    key_gain = jnp.clip(1.0 + 0.1 * jax.random.normal(arg_keys[9], (HEAD_SIZE,), jnp.float32), 0.5, 1.5)
    mlp_gain = jnp.clip(1.0 + 0.1 * jax.random.normal(arg_keys[10], (MODEL_WIDTH,), jnp.float32), 0.5, 1.5)
    router_weight = scatter_about(arg_keys[11], (MODEL_WIDTH, EXPERTS), (4 * MODEL_WIDTH) ** -0.5, 0.0625)
    gate_weight = scatter_about(arg_keys[12], (EXPERTS, MODEL_WIDTH, FF), MODEL_WIDTH ** -0.5, 0.125, ((0, 32), (2, 4)))
    up_weight = scatter_about(arg_keys[13], (EXPERTS, MODEL_WIDTH, FF), MODEL_WIDTH ** -0.5, 0.125, ((0, 32), (2, 4)))
    down_weight = scatter_about(arg_keys[14], (EXPERTS, FF, MODEL_WIDTH), (FF // 8) ** -0.5, 0.625, ((0, 32), (1, 4)))
    cotangent = scatter_about(arg_keys[15], (TOKENS, MODEL_WIDTH), 1.0, 6.0, ((0, 32),))
    return dict(tokens=tokens, doc_ids=doc_ids, routes=routes, query_weight=query_weight, key_matrix=key_matrix, value_matrix=value_matrix, output_weight=output_weight, attn_gain=attn_gain, query_gain=query_gain, key_gain=key_gain, mlp_gain=mlp_gain, router_weight=router_weight, gate_weight=gate_weight, up_weight=up_weight, down_weight=down_weight, cotangent=cotangent)


@jax.custom_vjp
def low_cast(v):
    return lax.optimization_barrier(v.astype(jnp.bfloat16)).astype(jnp.float32)

@jax.custom_vjp
def low_cast_back(v):
    return v

def low_keep(v):
    return (low_cast(v), None)

def low_pass(kept, grad):
    return (grad,)

def back_keep(v):
    return (v, None)

def back_low(kept, grad):
    return (low_cast(grad),)
low_cast.defvjp(low_keep, low_pass)
low_cast_back.defvjp(back_keep, back_low)
EPSILON = 1e-06
THETA = 1000000.0
MASKED = -1e+30
TOP_PRECISION = lax.Precision.HIGHEST

def rms_apply(value_rows, gain):
    return value_rows * lax.rsqrt(lax.optimization_barrier(jnp.mean(value_rows * value_rows, axis=-1, keepdims=True)) + EPSILON) * gain

def doc_positions(doc_row):
    count_of_rows = doc_row.shape[0]
    places = jnp.arange(count_of_rows, dtype=jnp.int32)
    starts_new = jnp.concatenate([jnp.ones((1,), jnp.bool_), doc_row[1:] != doc_row[:-1]])
    return places - lax.cummax(jnp.where(starts_new, places, 0), axis=0)

def rotate(value_rows, places):
    half_dim = value_rows.shape[-1] // 2
    inverse = THETA ** (-jnp.arange(half_dim, dtype=jnp.float32) * 2.0 / value_rows.shape[-1])
    angles = places.astype(jnp.float32)[:, None, None] * inverse[None, None, :]
    cosine = jnp.cos(angles)
    sine_table = jnp.sin(angles)
    first_half = value_rows[..., :half_dim]
    second_half = value_rows[..., half_dim:]
    return jnp.concatenate([first_half * cosine - second_half * sine_table, second_half * cosine + first_half * sine_table], axis=-1)

def attend_heads(sequence):
    query_tile_block, key_block, value_block, doc_row = sequence
    count_of_rows = query_tile_block.shape[0]
    group_width = QUERY_HEAD_COUNT // KEY_VALUE_HEADS
    grouped_heads = query_tile_block.reshape(count_of_rows, KEY_VALUE_HEADS, group_width, HEAD_SIZE)
    scores = low_cast_back(jnp.einsum('qkgd,skd->kgqs', grouped_heads, key_block, precision=TOP_PRECISION) * (1.0 / math.sqrt(HEAD_SIZE)))
    places = jnp.arange(count_of_rows, dtype=jnp.int32)
    allowed = (places[None, :] <= places[:, None]) & (doc_row[:, None] == doc_row[None, :])
    weights = low_cast(jax.nn.softmax(jnp.where(allowed[None, None], scores, MASKED), axis=-1))
    mixed_heads = jnp.einsum('kgqs,skd->qkgd', weights, value_block, precision=TOP_PRECISION)
    return mixed_heads.reshape(count_of_rows, QUERY_HEAD_COUNT * HEAD_SIZE)

def experts_mix(normed, gate_probs, routes, gate_weight, up_weight, down_weight):
    flat_routes = routes.reshape(-1)
    sorted_pairs = jnp.argsort(flat_routes, stable=True).astype(jnp.int32)
    expert_ids = jnp.arange(EXPERTS, dtype=jnp.int32)
    counts = lax.optimization_barrier(jnp.sum((flat_routes[:, None] == expert_ids[None, :]).astype(jnp.int32), axis=0))
    offsets = jnp.cumsum(counts) - counts
    room_rows = N_EP * CAP
    padded = jnp.concatenate([sorted_pairs, jnp.zeros((room_rows,), jnp.int32)])
    places = offsets[:, None] + jnp.arange(room_rows, dtype=jnp.int32)[None, :]
    pair_ids = padded[places]
    live_rows = jnp.arange(room_rows, dtype=jnp.int32)[None, :] < counts[:, None]
    owners = pair_ids // TOP
    weights = jnp.where(live_rows, gate_probs.reshape(-1)[pair_ids], 0.0)

    def one_expert(entry):
        gate_mat, up_mat, down_mat, row_owner = entry
        gathered = normed[row_owner]
        gate_val = low_cast_back(jnp.dot(gathered, gate_mat, precision=TOP_PRECISION))
        up_val = low_cast_back(jnp.dot(gathered, up_mat, precision=TOP_PRECISION))
        act = low_cast(jax.nn.silu(gate_val) * up_val)
        return low_cast_back(jnp.dot(act, down_mat, precision=TOP_PRECISION))
    expert_rows = lax.map(jax.checkpoint(one_expert), (gate_weight, up_weight, down_weight, owners))
    weighted = (weights[:, :, None] * expert_rows).reshape(-1, normed.shape[1])
    return jnp.zeros_like(normed).at[owners.reshape(-1)].add(weighted)

def layer_forward(tokens_wide, query_weight, key_matrix, value_matrix, output_weight, attn_gain, query_gain, key_gain, mlp_gain, router_weight, gate_weight, up_weight, down_weight, doc_ids, routes):
    total_tokens = tokens_wide.shape[0]
    first_normed_input = low_cast(rms_apply(tokens_wide, attn_gain))
    query_raw = low_cast_back(jnp.dot(first_normed_input, query_weight, precision=TOP_PRECISION)).reshape(total_tokens, QUERY_HEAD_COUNT, HEAD_SIZE)
    key_unrotated = low_cast_back(jnp.dot(first_normed_input, key_matrix, precision=TOP_PRECISION)).reshape(total_tokens, KEY_VALUE_HEADS, HEAD_SIZE)
    value_rows = low_cast(low_cast_back(jnp.dot(first_normed_input, value_matrix, precision=TOP_PRECISION))).reshape(total_tokens, KEY_VALUE_HEADS, HEAD_SIZE)
    document_rows = doc_ids.reshape(-1, SEQUENCE_LENGTH)
    places = jax.vmap(doc_positions)(document_rows).reshape(-1)
    query_rotated = low_cast(low_cast_back(rotate(rms_apply(query_raw, query_gain), places)))
    keys_rotated = low_cast(low_cast_back(rotate(rms_apply(key_unrotated, key_gain), places)))
    rows_per_head = lax.map(jax.checkpoint(attend_heads), (query_rotated.reshape(-1, SEQUENCE_LENGTH, QUERY_HEAD_COUNT, HEAD_SIZE), keys_rotated.reshape(-1, SEQUENCE_LENGTH, KEY_VALUE_HEADS, HEAD_SIZE), value_rows.reshape(-1, SEQUENCE_LENGTH, KEY_VALUE_HEADS, HEAD_SIZE), document_rows))
    rows_per_head = low_cast(low_cast_back(rows_per_head.reshape(total_tokens, QUERY_HEAD_COUNT * HEAD_SIZE)))
    attn_branch = low_cast_back(jnp.dot(rows_per_head, output_weight.T, precision=TOP_PRECISION))
    hidden = tokens_wide + attn_branch
    normed_second = low_cast(rms_apply(hidden, mlp_gain))
    logits = low_cast_back(jnp.dot(normed_second, router_weight, precision=TOP_PRECISION))
    gate_probs = jax.nn.softmax(jnp.take_along_axis(logits, routes, axis=1), axis=-1)
    return hidden + experts_mix(normed_second, gate_probs, routes, gate_weight, up_weight, down_weight)

def reference(tokens, doc_ids, routes, query_weight, key_matrix, value_matrix, output_weight, attn_gain, query_gain, key_gain, mlp_gain, router_weight, gate_weight, up_weight, down_weight, cotangent):
    widened = tuple((entry_value.astype(jnp.float32) for entry_value in (tokens, query_weight, key_matrix, value_matrix, output_weight, attn_gain, query_gain, key_gain, mlp_gain, router_weight, gate_weight, up_weight, down_weight)))

    def forward(*params):
        return layer_forward(*params, doc_ids, routes)
    layer_out, pullback = jax.vjp(forward, *widened)
    gradients = pullback(cotangent.astype(jnp.float32))
    return (layer_out.astype(jnp.bfloat16), gradients[0].astype(jnp.bfloat16), gradients[1], gradients[2], gradients[3], gradients[4], gradients[5], gradients[6], gradients[7], gradients[8], gradients[9], gradients[10], gradients[11], gradients[12])
```

```python
import math

import jax
import jax.numpy as jnp
from jax import lax
from jax.experimental import pallas as pl
from jax.experimental.pallas import tpu as pltpu
from jax.sharding import PartitionSpec as P

EPSILON = 1e-06
THETA = 1000000.0
MASKED = -1e30
BF = jnp.bfloat16
F32 = jnp.float32
COLS = (((1,), (1,)), ((), ()))
ROWS = (((0,), (0,)), ((), ()))


def norm_rate(value_rows):
    return lax.rsqrt(jnp.mean(value_rows * value_rows, axis=-1, keepdims=True) + EPSILON)


def norm_back(value_rows, rate, gain, upstream):
    scaled = upstream * gain
    inner = jnp.mean(scaled * value_rows, axis=-1, keepdims=True)
    return rate * scaled - value_rows * (rate * rate * rate) * inner


def rounded(value_rows):
    return lax.optimization_barrier(value_rows.astype(BF)).astype(F32)


def doc_positions(doc_row):
    count_of_rows = doc_row.shape[0]
    places = jnp.arange(count_of_rows, dtype=jnp.int32)
    starts_new = jnp.concatenate([jnp.ones((1,), jnp.bool_), doc_row[1:] != doc_row[:-1]])
    return places - lax.cummax(jnp.where(starts_new, places, 0), axis=0)


def rope_tables(places, head_dim):
    half_dim = head_dim // 2
    inverse = THETA ** (-jnp.arange(half_dim, dtype=F32) * 2.0 / head_dim)
    angles = places.astype(F32)[:, None, None] * inverse[None, None, :]
    return (jnp.cos(angles), jnp.sin(angles))


def rotate(value_rows, cosine, sine_table):
    half_dim = value_rows.shape[-1] // 2
    first_half = value_rows[..., :half_dim]
    second_half = value_rows[..., half_dim:]
    return jnp.concatenate(
        [
            first_half * cosine - second_half * sine_table,
            second_half * cosine + first_half * sine_table,
        ],
        axis=-1,
    )


def rotate_back(upstream, cosine, sine_table):
    return rotate(upstream, cosine, -sine_table)


def attention_scores(query_low, keys_low, doc_ids, score_scale):
    raw_scores = (
        jnp.einsum("qkgd,skd->kgqs", query_low, keys_low, preferred_element_type=F32) * score_scale
    )
    places = jnp.arange(keys_low.shape[0], dtype=jnp.int32)
    allowed = (places[None, :] <= places[:, None]) & (doc_ids[:, None] == doc_ids[None, :])
    return jnp.where(allowed[None, None], raw_scores, MASKED)


def split_low(value_rows):
    high = value_rows.astype(BF)
    return high, (value_rows - high.astype(F32)).astype(BF)


def after(value, *earlier):
    return lax.optimization_barrier((value,) + earlier)[0]


def ring(count, shift):
    return [(i, (i + shift) % count) for i in range(count)]


def row_block(value_rows, index, count):
    size = value_rows.shape[0] // count
    return lax.dynamic_slice_in_dim(value_rows, index * size, size, 0)


def tp_scatter(part):
    count, me = lax.axis_size("tp"), lax.axis_index("tp")
    total = row_block(part, me, count).astype(F32)
    for shift in range(1, count):
        block = row_block(part, (me + shift) % count, count)
        total = total + lax.ppermute(block, "tp", ring(count, shift)).astype(F32)
    return total


def tp_gather(block):
    count, me = lax.axis_size("tp"), lax.axis_index("tp")
    whole = jnp.zeros((count,) + block.shape, block.dtype)
    whole = lax.dynamic_update_index_in_dim(whole, block, me, 0)
    for shift in range(1, count):
        got = lax.ppermute(block, "tp", ring(count, shift))
        whole = lax.dynamic_update_index_in_dim(whole, got, (me - shift) % count, 0)
    return whole.reshape((-1,) + block.shape[1:])


def tp_sum_blocks(blocks):
    count = lax.axis_size("tp")
    total = blocks[0].astype(F32)
    for shift in range(1, count):
        total = total + lax.ppermute(blocks[shift], "tp", ring(count, shift)).astype(F32)
    return total


def project_kernel(count, columns, steps, left_ref, *refs):
    rights, outs, held = refs[: len(columns)], refs[len(columns) : -1], refs[-1]
    me = lax.axis_index("tp")
    size = left_ref.shape[0] // count
    for right_ref, (first, by_rows) in zip(rights, columns):
        part = left_ref[:, first : first + right_ref.shape[1 - by_rows]]
        got = lax.dot_general(
            part, right_ref[...], COLS if not by_rows else (((1,), (0,)), ((), ())), preferred_element_type=F32
        )
        if first == 0:
            held[...] = got
        else:
            held[...] += got
    for shift in range(count):
        start = pl.multiple_of((me + shift) % count * size, size)
        outs[shift][...] = held[pl.ds(start, size), :].astype(BF)


def project(left, rights, by_rows, tile):
    count = lax.axis_size("tp")
    length = left.shape[0]
    width = rights[0].shape[1 if by_rows else 0]
    columns, first = [], 0
    for right in rights:
        columns.append((first, int(by_rows)))
        first += right.shape[0 if by_rows else 1]
    tile = min(tile, width)
    steps = width // tile
    in_specs = [pl.BlockSpec(left.shape, lambda i: (0, 0))]
    for right in rights:
        in_specs.append(
            pl.BlockSpec((right.shape[0], tile), lambda i: (0, i))
            if by_rows
            else pl.BlockSpec((tile, right.shape[1]), lambda i: (i, 0))
        )
    size = length // count
    return pl.pallas_call(
        lambda *refs: project_kernel(count, columns, steps, *refs),
        grid=(steps,),
        in_specs=in_specs,
        out_specs=[pl.BlockSpec((size, tile), lambda i: (0, i))] * count,
        out_shape=[jax.ShapeDtypeStruct((size, width), BF)] * count,
        scratch_shapes=[pltpu.VMEM((length, tile), F32)],
        compiler_params=pltpu.CompilerParams(vmem_limit_bytes=40 * 2**20),
        cost_estimate=pl.CostEstimate(
            flops=2 * length * first * width,
            bytes_accessed=2 * (length * first + first * width + length * width),
            transcendentals=0,
        ),
    )(left, *rights)


def expert_kernel(
    width, rows_ref, grads_ref, *refs
):
    count = (len(refs) - 8) // 3
    sources = [refs[k * count : (k + 1) * count] for k in range(3)]
    back_ref, act_ref, gate_back_ref, up_back_ref = refs[3 * count : 3 * count + 4]
    held, sems = refs[3 * count + 4 : 3 * count + 7], refs[3 * count + 7]
    size = sources[0][0].shape[0]

    def loads(which):
        return [
            pltpu.make_async_copy(
                source, held[which].at[pl.ds(part * size, size), :], sems.at[which, part]
            )
            for part, source in enumerate(sources[which])
        ]

    first = pl.program_id(0) == 0

    @pl.when(first)
    def _():
        for which in range(3):
            for load in loads(which):
                load.start()
        for load in loads(0):
            load.wait()

    rows = rows_ref[...]
    gate_val = lax.dot_general(rows, held[0][...], COLS, preferred_element_type=F32)

    @pl.when(first)
    def _():
        for load in loads(1):
            load.wait()

    up_val = lax.dot_general(rows, held[1][...], COLS, preferred_element_type=F32)

    @pl.when(first)
    def _():
        for load in loads(2):
            load.wait()

    act_grad = lax.dot_general(grads_ref[...], held[2][...], COLS, preferred_element_type=F32)
    gate_sig = jax.nn.sigmoid(gate_val)
    gate_act = gate_val * gate_sig
    act_low = (gate_act * up_val).astype(BF)
    act_ref[...] = act_low
    gate_back = (act_grad * up_val * gate_sig * (1.0 + gate_val * (1.0 - gate_sig))).astype(BF)
    up_back = (act_grad * gate_act).astype(BF)
    gate_back_ref[...] = gate_back
    up_back_ref[...] = up_back
    slot_grad = jnp.sum(act_low.astype(F32) * act_grad, axis=1, keepdims=True)
    back_ref[:, width:] = jnp.broadcast_to(
        slot_grad, (rows.shape[0], back_ref.shape[1] - width)
    ).astype(BF)
    back_ref[:, :width] = (
        jnp.dot(gate_back, held[0][...], preferred_element_type=F32)
        + jnp.dot(up_back, held[1][...], preferred_element_type=F32)
    ).astype(BF)


def expert_pass(rows_in, grads_in, gates, ups, downs, extra, tile=512):
    slots, width = rows_in.shape
    tile = min(tile, slots)
    hidden = len(gates) * gates[0].shape[0]
    tall = pl.BlockSpec((tile, width), lambda i: (i, 0))
    narrow = pl.BlockSpec((tile, hidden), lambda i: (i, 0))
    low = jax.ShapeDtypeStruct((slots, hidden), BF)
    return pl.pallas_call(
        lambda *refs: expert_kernel(width, *refs),
        grid=(slots // tile,),
        in_specs=[tall, tall] + [pl.BlockSpec(memory_space=pl.ANY)] * (3 * len(gates)),
        out_specs=[pl.BlockSpec((tile, width + extra), lambda i: (i, 0)), narrow, narrow, narrow],
        out_shape=[jax.ShapeDtypeStruct((slots, width + extra), BF), low, low, low],
        scratch_shapes=[pltpu.VMEM((hidden, width), BF)] * 3
        + [pltpu.SemaphoreType.DMA((3, len(gates)))],
        compiler_params=pltpu.CompilerParams(vmem_limit_bytes=56 * 2**20),
        cost_estimate=pl.CostEstimate(
            flops=10 * slots * width * hidden,
            bytes_accessed=6 * slots * width + 6 * width * hidden,
            transcendentals=slots * hidden,
        ),
    )(rows_in, grads_in, *gates, *ups, *downs)


def place_kernel(count, *refs):
    ins, out_ref = refs[:count], refs[count]
    step = pl.program_id(0)
    for shift in range(count):

        @pl.when(step == shift)
        def _():
            out_ref[0] = ins[shift][...].astype(out_ref.dtype)


def place_blocks(blocks, direction, dtype, tile):
    count, me = len(blocks), lax.axis_index("tp")
    rows, cols = blocks[0].shape
    steps = rows // tile

    def held(shift):
        return lambda s, t, me_ref: (jnp.where(s < shift, 0, jnp.where(s > shift, steps - 1, t)), 0)

    return pl.pallas_call(
        lambda me_ref, *refs: place_kernel(count, *refs),
        grid_spec=pltpu.PrefetchScalarGridSpec(
            num_scalar_prefetch=1,
            grid=(count, steps),
            in_specs=[pl.BlockSpec((tile, cols), held(shift)) for shift in range(count)],
            out_specs=pl.BlockSpec(
                (1, tile, cols), lambda s, t, me_ref: ((me_ref[0] + direction * s + count) % count, t, 0)
            ),
        ),
        out_shape=jax.ShapeDtypeStruct((count, rows, cols), dtype),
        cost_estimate=pl.CostEstimate(
            flops=0, bytes_accessed=count * rows * cols * (2 + jnp.dtype(dtype).itemsize), transcendentals=0
        ),
    )(me.astype(jnp.int32).reshape(1), *blocks)


def expert_pull(weight, shifts=None):
    count, me = lax.axis_size("tp"), lax.axis_index("tp")
    blocks = []
    for shift in range(count) if shifts is None else shifts:
        block = lax.dynamic_index_in_dim(weight, (me + shift) % count, 0, keepdims=False)
        blocks.append(lax.ppermute(block, "tp", ring(count, shift)) if shift else block)
    return blocks


def expert_push(grad):
    count = lax.axis_size("tp")
    size = grad.shape[0] // count
    blocks = [grad[:size]]
    for shift in range(1, count):
        block = grad[shift * size : (shift + 1) * size]
        blocks.append(lax.ppermute(block, "tp", ring(count, -shift)))
    return place_blocks(blocks, 1, F32, size)


def ep_exchange(rows):
    return lax.all_to_all(rows, "ep", 0, 0, tiled=True)


def wgrad_kernel(share, spans, *refs):
    count = len(spans)
    lefts, rights, (keep_ref, send_ref, held) = refs[:count], refs[count : 2 * count], refs[2 * count :]
    core = lax.axis_index("ep") % 2
    for left_ref, right_ref, (first, size) in zip(lefts, rights, spans):
        held[:, first : first + size] = lax.dot_general(
            left_ref[...], right_ref[...], ROWS, preferred_element_type=F32
        )
    for chip in range(held.shape[0] // (2 * share)):
        kept = pl.multiple_of((2 * chip + core) * share, share)
        sent = pl.multiple_of((2 * chip + 1 - core) * share, share)
        keep_ref[chip * share : (chip + 1) * share, :] = held[pl.ds(kept, share), :]
        send_ref[chip * share : (chip + 1) * share, :] = held[pl.ds(sent, share), :].astype(BF)


def ep_grad_sum(pairs, tile=512):
    count = lax.axis_size("ep")
    length, width = pairs[0][0].shape
    share = width // count
    tile = min(tile, width)
    spans, cols = [], 0
    for _, right in pairs:
        spans.append((cols, right.shape[1]))
        cols += right.shape[1]
    half = pl.BlockSpec((tile // 2, cols), lambda i: (i, 0))
    keep, send = pl.pallas_call(
        lambda *refs: wgrad_kernel(share, spans, *refs),
        grid=(width // tile,),
        in_specs=[pl.BlockSpec((length, tile), lambda i: (0, i))] * len(pairs)
        + [pl.BlockSpec(right.shape, lambda i: (0, 0)) for _, right in pairs],
        out_specs=[half, half],
        out_shape=[
            jax.ShapeDtypeStruct((width // 2, cols), F32),
            jax.ShapeDtypeStruct((width // 2, cols), BF),
        ],
        scratch_shapes=[pltpu.VMEM((tile, cols), F32)],
        compiler_params=pltpu.CompilerParams(vmem_limit_bytes=40 * 2**20),
        cost_estimate=pl.CostEstimate(
            flops=2 * length * width * cols, bytes_accessed=3 * width * cols, transcendentals=0
        ),
    )(*[left for left, _ in pairs], *[right for _, right in pairs])
    got = lax.ppermute(send, "ep", [(i, i ^ 1) for i in range(count)])
    pair = (keep + got.astype(F32)).astype(BF).reshape(count // 2, share, cols)
    if count > 2:
        groups = [list(range(core, count, 2)) for core in range(2)]
        pair = lax.all_to_all(pair, "ep", 0, 0, axis_index_groups=groups, tiled=True)
    return jnp.sum(pair.astype(F32), axis=0)


def combine_kernel(count, width, weight_ref, mask_ref, rows_ref, column_ref, *refs):
    outs, held = refs[:-1], refs[-1]
    size = weight_ref.shape[0] // count
    held[:, :width] = jnp.dot(weight_ref[...], rows_ref[:, :width], preferred_element_type=F32)
    held[:, width:] = jnp.dot(
        mask_ref[...], rows_ref[:, width:] * column_ref[...], preferred_element_type=F32
    )
    for shift in range(count):
        outs[shift][...] = held[shift * size : (shift + 1) * size, :].astype(BF)


def combine(weights, mask, rows, slot_columns, count):
    length, wide = weights.shape[0], rows.shape[1]
    return pl.pallas_call(
        lambda *refs: combine_kernel(count, wide - slot_columns.shape[1], *refs),
        out_shape=[jax.ShapeDtypeStruct((length // count, wide), BF)] * count,
        scratch_shapes=[pltpu.VMEM((length, wide), F32)],
        compiler_params=pltpu.CompilerParams(vmem_limit_bytes=40 * 2**20),
        cost_estimate=pl.CostEstimate(
            flops=2 * length * rows.shape[0] * wide, bytes_accessed=2 * rows.shape[0] * wide, transcendentals=0
        ),
    )(weights, mask, rows, slot_columns)


def sum_everywhere(value):
    tp_count, ep_count = lax.axis_size("tp"), lax.axis_size("ep")
    levels, stride = [], 1
    for size in (2, 4, 4):
        if stride < ep_count:
            levels.append((stride, min(size, ep_count // stride)))
            stride *= levels[-1][1]
    total = value
    for shift in range(1, tp_count):
        total = total + lax.ppermute(value, "tp", ring(tp_count, shift))
    for stride, size in levels:
        value = total
        for shift in range(1, size):
            moves = [
                (i, i - i // stride % size * stride + (i // stride + shift) % size * stride)
                for i in range(ep_count)
            ]
            total = total + lax.ppermute(value, "ep", moves)
    return total


def per_device(
    tokens,
    doc_ids,
    routes,
    query_weight,
    key_matrix,
    value_matrix,
    output_weight,
    attn_gain,
    query_gain,
    key_gain,
    mlp_gain,
    router_weight,
    gate_weight,
    up_weight,
    down_weight,
    cotangent,
):
    length, width = tokens.shape
    head_dim = query_gain.shape[0]
    query_heads = query_weight.shape[1] // head_dim
    kv_heads = key_matrix.shape[1] // head_dim
    group_width = query_heads // kv_heads
    score_scale = 1.0 / math.sqrt(head_dim)
    total_experts = router_weight.shape[1]
    top_count = routes.shape[1]
    ep_count, tp_count = lax.axis_size("ep"), lax.axis_size("tp")
    ep_index, tp_index = lax.axis_index("ep"), lax.axis_index("tp")
    capacity = length * top_count * 4 // (3 * total_experts)
    slots = ep_count * capacity

    gate_rows = jnp.swapaxes(gate_weight, 1, 2)
    up_rows = jnp.swapaxes(up_weight, 1, 2)
    gates = expert_pull(gate_rows)
    near_ups = expert_pull(up_rows, (0, 1, 3))

    routes_by_class = routes % tp_count * ep_count + routes // tp_count
    columns = jnp.arange(total_experts, dtype=jnp.int32)
    routed = jnp.any(routes_by_class[:, :, None] == columns[None, None, :], axis=1)
    own_routed = lax.dynamic_slice_in_dim(routed, tp_index * ep_count, ep_count, 1)
    line = jnp.arange(length, dtype=jnp.int32)
    earlier = (line[:, None] > line[None, :]).astype(BF)
    rank = jnp.dot(earlier, own_routed.astype(BF), preferred_element_type=F32).astype(jnp.int32)
    places = jnp.where(own_routed, rank, -1)
    slot_line = jnp.arange(slots, dtype=jnp.int32)
    slot_owner = (slot_line[None, :] // capacity == jnp.arange(ep_count, dtype=jnp.int32)[:, None]).astype(BF)
    place_wide = jnp.dot(places.astype(BF), slot_owner, preferred_element_type=F32)
    send_mask = (place_wide == (slot_line % capacity).astype(F32)[None, :]).astype(BF)

    def fill_slots(rows):
        return lax.dot_general(send_mask, rows, ROWS, preferred_element_type=F32).astype(BF)

    def dispatch(sent):
        return ep_exchange(sent.reshape(ep_count, capacity, -1)).reshape(slots, -1)

    sent_grads = fill_slots(jnp.concatenate([cotangent, routed.astype(BF)], axis=1))
    grads_in = dispatch(sent_grads)
    tokens = after(tokens, sent_grads)

    inputs_wide = tokens.astype(F32)
    rate_first = norm_rate(inputs_wide)
    first_normed_input = (inputs_wide * rate_first * attn_gain).astype(BF)
    query_raw = jnp.dot(first_normed_input, query_weight, preferred_element_type=F32).reshape(
        length, query_heads, head_dim
    )
    key_unrotated = jnp.dot(first_normed_input, key_matrix, preferred_element_type=F32).reshape(
        length, kv_heads, head_dim
    )
    values_low = (
        jnp.dot(first_normed_input, value_matrix, preferred_element_type=F32)
        .astype(BF)
        .reshape(length, kv_heads, head_dim)
    )
    cosine, sine_table = rope_tables(doc_positions(doc_ids), head_dim)
    query_rate = norm_rate(query_raw)
    key_rate = norm_rate(key_unrotated)
    query_low = (
        rotate(query_raw * query_rate * query_gain, cosine, sine_table)
        .astype(BF)
        .reshape(length, kv_heads, group_width, head_dim)
    )
    keys_low = rotate(key_unrotated * key_rate * key_gain, cosine, sine_table).astype(BF)
    masked = attention_scores(query_low, keys_low, doc_ids, score_scale)
    row_max = jnp.max(masked, axis=-1, keepdims=True)
    exp_scores = jnp.exp(masked - row_max)
    row_total = jnp.sum(exp_scores, axis=-1, keepdims=True)
    weights_low = (exp_scores / row_total).astype(BF)
    heads_low = (
        jnp.einsum("kgqs,skd->qkgd", weights_low, values_low, preferred_element_type=F32)
        .reshape(length, query_heads * head_dim)
        .astype(BF)
    )
    log_total = row_max + jnp.log(row_total)
    attn_part = project(after(heads_low, *gates, *near_ups), [output_weight], False, 512)

    tokens_own = row_block(inputs_wide, tp_index, tp_count)
    upstream_own = row_block(cotangent, tp_index, tp_count).astype(F32)
    hidden = tokens_own + tp_sum_blocks(attn_part)
    rate_second = norm_rate(hidden)
    normed_own = (hidden * rate_second * mlp_gain).astype(BF)
    normed_second = tp_gather(normed_own)
    rows_in = dispatch(after(fill_slots(normed_second), grads_in))
    far_up = expert_pull(after(up_rows, normed_second), (2,))
    ups = [near_ups[0], near_ups[1], far_up[0], near_ups[2]]
    downs = expert_pull(after(down_weight, far_up[0]))
    down_full = jnp.concatenate(downs, axis=0)

    router_by_class = (
        router_weight.reshape(width, ep_count, tp_count).swapaxes(1, 2).reshape(width, total_experts)
    )
    logits = jnp.dot(normed_second, router_by_class, preferred_element_type=F32)
    logits = jnp.where(routed, logits, MASKED)
    exp_logits = jnp.exp(logits - jnp.max(logits, axis=-1, keepdims=True))
    gate_probs = exp_logits / jnp.sum(exp_logits, axis=-1, keepdims=True)
    own_probs = lax.dynamic_slice_in_dim(gate_probs, tp_index * ep_count, ep_count, 1)
    probs_high, probs_low = split_low(own_probs)
    probs_wide = jnp.dot(probs_high, slot_owner, preferred_element_type=F32) + jnp.dot(
        probs_low, slot_owner, preferred_element_type=F32
    )
    weigh_back = (probs_wide * send_mask.astype(F32)).astype(BF)

    rows_grad, act_low, gate_back, up_back = expert_pass(
        rows_in, grads_in, gates, ups, downs, total_experts
    )
    back_rows = dispatch(rows_grad)
    expert_out = jnp.dot(act_low, down_full, preferred_element_type=F32).astype(BF)
    returned = dispatch(after(expert_out, back_rows))

    slot_logits = jnp.dot(rows_in, router_by_class, preferred_element_type=F32)
    slot_logits = jnp.where(grads_in[:, width:].astype(F32) > 0.5, slot_logits, MASKED)
    slot_exp = jnp.exp(slot_logits - jnp.max(slot_logits, axis=-1, keepdims=True))
    own_column = (columns == tp_index * ep_count + ep_index).astype(F32)
    probs_in = jnp.sum(slot_exp * own_column[None, :], axis=-1) / jnp.sum(slot_exp, axis=-1)

    def weighed(value):
        return (value.astype(F32) * probs_in[:, None]).astype(BF)

    def expert_grad(left, right):
        return lax.dot_general(weighed(left), right, ROWS, preferred_element_type=F32).astype(BF)

    down_wgrad = expert_push(expert_grad(act_low, grads_in[:, :width]))
    gate_part = expert_grad(gate_back, rows_in)
    up_part = expert_grad(up_back, rows_in)

    rows_by_peer = jnp.roll(weigh_back, -tp_index * (length // tp_count), axis=0)
    mask_by_peer = jnp.roll(send_mask, -tp_index * (length // tp_count), axis=0)
    slot_columns = slot_line[:, None] // capacity + tp_index * ep_count == columns[None, :]
    input_parts = combine(rows_by_peer, mask_by_peer, back_rows, slot_columns.astype(BF), tp_count)
    back_sum = tp_sum_blocks(input_parts)

    gate_grad = back_sum[:, width:]
    probs_own = row_block(gate_probs, tp_index, tp_count)
    gate_mean = jnp.sum(probs_own * gate_grad, axis=-1, keepdims=True)
    logit_own = (probs_own * (gate_grad - gate_mean)).astype(BF)
    router_input = lax.dot_general(logit_own, router_by_class, COLS, preferred_element_type=F32)
    second_grad = router_input + back_sum[:, :width]
    mlp_gain_part = jnp.sum(second_grad * hidden * rate_second, axis=0)
    hidden_grad = upstream_own + norm_back(hidden, rate_second, mlp_gain, second_grad)
    branch_low = tp_gather(hidden_grad.astype(BF))
    logit_grad = tp_gather(after(logit_own, branch_low))
    heads_grad = (
        jnp.dot(branch_low, output_weight, preferred_element_type=F32)
        .astype(BF)
        .reshape(length, kv_heads, group_width, head_dim)
    )

    gate_wgrad = jnp.swapaxes(expert_push(after(gate_part, branch_low)), 1, 2)
    up_wgrad = jnp.swapaxes(expert_push(after(up_part, branch_low)), 1, 2)

    mix_part = jnp.dot(weigh_back, after(returned, branch_low), preferred_element_type=F32)
    mix_own = lax.psum_scatter(mix_part.astype(BF), "tp", scatter_dimension=0, tiled=True)
    layer_own = (hidden + mix_own.astype(F32)).astype(BF)
    layer_out = lax.all_gather(layer_own, "tp", axis=0, tiled=True)

    later_wgrad = ep_grad_sum(
        [(branch_low, after(heads_low, returned)), (normed_second, logit_grad)]
    )
    output_wgrad, router_wgrad = later_wgrad[:, : heads_low.shape[1]], later_wgrad[:, heads_low.shape[1] :]
    router_wgrad = (
        router_wgrad.reshape(-1, tp_count, ep_count).swapaxes(1, 2).reshape(-1, total_experts)
    )

    masked = attention_scores(query_low, keys_low, doc_ids, score_scale)
    probs = jnp.exp(masked - log_total)
    prob_grad = jnp.einsum("qkgd,skd->kgqs", heads_grad, values_low, preferred_element_type=F32)
    delta = jnp.sum(probs * prob_grad, axis=-1, keepdims=True)
    score_grad = (probs * (prob_grad - delta)).astype(BF)
    value_accum = jnp.einsum(
        "kgqs,qkgd->skd", probs.astype(BF), heads_grad, preferred_element_type=F32
    )
    key_accum = (
        jnp.einsum("kgqs,qkgd->skd", score_grad, query_low, preferred_element_type=F32)
        * score_scale
    )
    query_accum = (
        jnp.einsum("kgqs,skd->qkgd", score_grad, keys_low, preferred_element_type=F32) * score_scale
    )
    query_back = rounded(query_accum.reshape(length, query_heads, head_dim))
    key_back = rounded(key_accum)
    query_norm_grad = rotate_back(query_back, cosine, sine_table)
    key_norm_grad = rotate_back(key_back, cosine, sine_table)
    query_gain_part = jnp.sum(query_norm_grad * query_raw * query_rate, axis=(0, 1))
    key_gain_part = jnp.sum(key_norm_grad * key_unrotated * key_rate, axis=(0, 1))
    query_raw_grad = (
        norm_back(query_raw, query_rate, query_gain, query_norm_grad)
        .astype(BF)
        .reshape(length, query_heads * head_dim)
    )
    key_raw_grad = (
        norm_back(key_unrotated, key_rate, key_gain, key_norm_grad)
        .astype(BF)
        .reshape(length, kv_heads * head_dim)
    )
    value_back = value_accum.astype(BF).reshape(length, kv_heads * head_dim)

    raw_grads = jnp.concatenate([query_raw_grad, key_raw_grad, value_back], axis=1)
    raw_wgrad = ep_grad_sum([(first_normed_input, after(raw_grads, output_wgrad))])
    query_cols, key_cols = query_weight.shape[1], key_matrix.shape[1]
    query_wgrad = raw_wgrad[:, :query_cols]
    key_wgrad = raw_wgrad[:, query_cols : query_cols + key_cols]
    value_wgrad = raw_wgrad[:, query_cols + key_cols :]

    first_parts = project(raw_grads, [query_weight, key_matrix, value_matrix], False, 512)
    first_grad = tp_sum_blocks(first_parts)
    rate_own = row_block(rate_first, tp_index, tp_count)
    attn_gain_part = jnp.sum(first_grad * tokens_own * rate_own, axis=0)
    gain_total = sum_everywhere(
        jnp.concatenate([attn_gain_part, mlp_gain_part, query_gain_part, key_gain_part]).reshape(
            -1, 128
        )
    ).reshape(-1)
    share = width // ep_count
    attn_gain_grad = lax.dynamic_slice_in_dim(gain_total, ep_index * share, share)
    mlp_gain_grad = lax.dynamic_slice_in_dim(gain_total, width + ep_index * share, share)
    query_gain_grad = gain_total[2 * width : 2 * width + head_dim]
    key_gain_grad = gain_total[2 * width + head_dim :]
    tokens_grad = tp_gather(
        (hidden_grad + norm_back(tokens_own, rate_own, attn_gain, first_grad)).astype(BF)
    )
    return (
        layer_out,
        tokens_grad,
        query_wgrad,
        key_wgrad,
        value_wgrad,
        output_wgrad,
        attn_gain_grad,
        query_gain_grad,
        key_gain_grad,
        mlp_gain_grad,
        router_wgrad,
        gate_wgrad,
        up_wgrad,
        down_wgrad,
    )


def solution(mesh):
    in_specs = (
        P("ep", None),
        P("ep"),
        P("ep", None),
        P(None, "tp"),
        P(None, "tp"),
        P(None, "tp"),
        P(None, "tp"),
        P(),
        P(),
        P(),
        P(),
        P(),
        P("ep", None, "tp"),
        P("ep", None, "tp"),
        P("ep", "tp", None),
        P("ep", None),
    )
    out_specs = (
        P("ep", None),
        P("ep", None),
        P("ep", "tp"),
        P("ep", "tp"),
        P("ep", "tp"),
        P("ep", "tp"),
        P("ep"),
        P(),
        P(),
        P("ep"),
        P("ep", None),
        P("ep", None, "tp"),
        P("ep", None, "tp"),
        P("ep", "tp", None),
    )
    return jax.shard_map(
        per_device, mesh=mesh, in_specs=in_specs, out_specs=out_specs, check_vma=False
    )
```

```python
import math

import jax
import jax.numpy as jnp
from jax import lax
from jax.experimental import pallas as pl
from jax.experimental.pallas import tpu as pltpu
from jax.sharding import PartitionSpec as P

EPSILON = 1e-06
THETA = 1000000.0
MASKED = -1e30
PROJECT_FIRST, PROJECT_LAST = 100.0, 1.0
HALVES_FIRST, HALVES_LATER = 0.1, 100.0
BF = jnp.bfloat16
F32 = jnp.float32
COLS = (((1,), (1,)), ((), ()))
ROWS = (((0,), (0,)), ((), ()))


def norm_rate(value_rows):
    return lax.rsqrt(jnp.mean(value_rows * value_rows, axis=-1, keepdims=True) + EPSILON)


def norm_back(value_rows, rate, gain, upstream):
    scaled = upstream * gain
    inner = jnp.mean(scaled * value_rows, axis=-1, keepdims=True)
    return rate * scaled - value_rows * (rate * rate * rate) * inner


def rope_tables(doc_ids, head_dim):
    half_dim = head_dim // 2
    starts = jnp.sum((doc_ids[None, :] < doc_ids[:, None]).astype(jnp.int32), axis=1)
    places = jnp.arange(doc_ids.shape[0], dtype=jnp.int32) - starts
    inverse = THETA ** (-jnp.arange(half_dim, dtype=F32) * 2.0 / head_dim)
    angles = places.astype(F32)[:, None] * inverse[None, :]
    cosine, sine = jnp.cos(angles), jnp.sin(angles)
    return (
        jnp.concatenate([cosine, cosine], axis=1),
        jnp.concatenate([-sine, sine], axis=1),
    )


def fixed(shape):
    return pl.BlockSpec(shape, lambda i: (0,) * len(shape))


def cost(flops, bytes_accessed, weight=1.0):
    return pl.CostEstimate(
        flops=int(flops * weight) + 1, bytes_accessed=int(bytes_accessed * weight) + 1, transcendentals=0
    )


def joined(*groups):
    flat = lax.optimization_barrier(tuple(value for group in groups for value in group))
    result, at = [], 0
    for group in groups:
        result.append(list(flat[at : at + len(group)]))
        at += len(group)
    return result


def params():
    return pltpu.CompilerParams(vmem_limit_bytes=60 * 2**20)


def turn(rows, cos, sin):
    return rows * cos + pltpu.roll(rows, rows.shape[1] // 2, 1) * sin


def turn_back(rows, cos, sin):
    return rows * cos - pltpu.roll(rows, rows.shape[1] // 2, 1) * sin


def attend_kernel(
    head_dim, scale,
    tokens_ref, gain_ref, query_ref, key_ref, value_ref, column_ref, row_ref, cos_ref, sin_ref, query_gain_ref, key_gain_ref,
    normed_ref, rate_ref, heads_ref, query_raw_ref, query_low_ref, probs_ref, key_raw_ref, key_low_ref, value_low_ref,
    bias_ref, value_turned_ref,
):
    length = tokens_ref.shape[0]

    @pl.when(pl.program_id(0) == 0)
    def _():
        wide = tokens_ref[...].astype(F32)
        rate = norm_rate(wide)
        rate_ref[...] = jnp.broadcast_to(rate, rate_ref.shape)
        normed_ref[...] = (wide * rate * gain_ref[...]).astype(BF)
        keys = jnp.dot(normed_ref[...], key_ref[...], preferred_element_type=F32)
        key_raw_ref[...] = keys
        key_low_ref[...] = turn(
            keys * norm_rate(keys) * key_gain_ref[...], cos_ref[...], sin_ref[...]
        ).astype(BF)
        values = jnp.dot(normed_ref[...], value_ref[...], preferred_element_type=F32)
        value_low_ref[...] = values.astype(BF)
        value_turned_ref[...] = values.T.astype(BF)
        key_place = lax.broadcasted_iota(jnp.int32, (length, length), 0)
        query_place = lax.broadcasted_iota(jnp.int32, (length, length), 1)
        allowed = (key_place <= query_place) & (column_ref[...] == row_ref[...])
        bias_ref[...] = jnp.where(allowed, 0.0, MASKED)

    query_raw = jnp.dot(normed_ref[...], query_ref[...], preferred_element_type=F32)
    query_raw_ref[...] = query_raw
    for head in range(query_raw.shape[1] // head_dim):
        span = slice(head * head_dim, (head + 1) * head_dim)
        query = query_raw[:, span]
        query_low = turn(
            query * norm_rate(query) * query_gain_ref[...], cos_ref[...], sin_ref[...]
        ).astype(BF)
        query_low_ref[:, span] = query_low
        scores = (
            lax.dot_general(key_low_ref[...], query_low, COLS, preferred_element_type=F32) * scale
            + bias_ref[...]
        )
        exps = jnp.exp(scores - jnp.max(scores, axis=0, keepdims=True))
        probs = exps * (1.0 / jnp.sum(exps, axis=0, keepdims=True))
        probs_ref[head] = probs
        mixed = jnp.dot(value_turned_ref[...], probs.astype(BF), preferred_element_type=F32)
        heads_ref[:, span] = mixed.T.astype(BF)


def attend(
    tokens, doc_ids, query_weight, key_matrix, value_matrix, attn_gain, query_gain, key_gain, cos, sin, weight=1.0
):
    length, width = tokens.shape
    head_dim = query_gain.shape[0]
    cols = query_weight.shape[1]
    step = min(2 * head_dim, cols)
    heads = cols // head_dim
    narrow = pl.BlockSpec((length, step), lambda i: (0, i))
    single = fixed((length, head_dim))
    return pl.pallas_call(
        lambda *refs: attend_kernel(head_dim, 1.0 / math.sqrt(head_dim), *refs),
        grid=(cols // step,),
        in_specs=[
            fixed((length, width)), fixed((1, width)),
            pl.BlockSpec((width, step), lambda i: (0, i)),
            fixed((width, head_dim)), fixed((width, head_dim)),
            fixed((length, 1)), fixed((1, length)), single, single,
            fixed((1, head_dim)), fixed((1, head_dim)),
        ],
        out_specs=[
            fixed((length, width)), single, narrow, narrow, narrow,
            pl.BlockSpec((step // head_dim, length, length), lambda i: (i, 0, 0)),
            single, single, single,
        ],
        out_shape=[
            jax.ShapeDtypeStruct((length, width), BF),
            jax.ShapeDtypeStruct((length, head_dim), F32),
            jax.ShapeDtypeStruct((length, cols), BF),
            jax.ShapeDtypeStruct((length, cols), F32),
            jax.ShapeDtypeStruct((length, cols), BF),
            jax.ShapeDtypeStruct((heads, length, length), F32),
            jax.ShapeDtypeStruct((length, head_dim), F32),
            jax.ShapeDtypeStruct((length, head_dim), BF),
            jax.ShapeDtypeStruct((length, head_dim), BF),
        ],
        scratch_shapes=[pltpu.VMEM((length, length), F32), pltpu.VMEM((head_dim, length), BF)],
        compiler_params=params(),
        cost_estimate=cost(2 * length * width * cols, 2 * width * cols, weight),
    )(
        tokens, attn_gain[None, :], query_weight, key_matrix, value_matrix,
        doc_ids[:, None], doc_ids[None, :], cos, sin, query_gain[None, :], key_gain[None, :],
    )


def norm_parts(raw, gain, upstream):
    rate = norm_rate(raw)
    gain_grad = jnp.sum(upstream * raw * rate, axis=0, keepdims=True)
    return norm_back(raw, rate, gain, upstream), gain_grad


def gather_rows(blocks, *whole_refs):
    count, me = len(blocks), lax.axis_index("tp")
    size = blocks[0].shape[0]
    for shift, block in enumerate(blocks):
        start = pl.multiple_of((me + count - shift) % count * size, size)
        first = 0
        for whole_ref in whole_refs:
            last = first + whole_ref.shape[1]
            whole_ref[pl.ds(start, size), :] = block[:, first:last]
            first = last


def attend_back_kernel(
    count, head_dim, scale, *refs
):
    blocks = refs[:count]
    (
        out_ref, query_raw_ref, query_low_ref, probs_ref, key_raw_ref, key_low_ref, value_low_ref, cos_ref, sin_ref, query_gain_ref, key_gain_ref,
        branch_ref, logit_ref, grads_ref, gains_ref,
        key_turned_ref, key_sum, value_sum,
    ) = refs[count:]
    step = pl.program_id(0)
    cols = query_raw_ref.shape[1]

    @pl.when(step == 0)
    def _():
        gather_rows(blocks, branch_ref, logit_ref)
        key_turned_ref[...] = key_low_ref[...].astype(F32).T.astype(BF)
        key_sum[...] = jnp.zeros_like(key_sum)
        value_sum[...] = jnp.zeros_like(value_sum)
        gains_ref[...] = jnp.zeros_like(gains_ref)

    heads_grad = jnp.dot(branch_ref[...], out_ref[...], preferred_element_type=F32).astype(BF)
    cos, sin = cos_ref[...], sin_ref[...]
    for head in range(cols // head_dim):
        span = slice(head * head_dim, (head + 1) * head_dim)
        upstream = heads_grad[:, span]
        probs = probs_ref[head]
        prob_grad = lax.dot_general(
            value_low_ref[...], upstream, COLS, preferred_element_type=F32
        )
        delta = jnp.sum(probs * prob_grad, axis=0, keepdims=True)
        score_grad = (probs * (prob_grad - delta)).astype(BF)
        value_sum[...] += jnp.dot(probs.astype(BF), upstream, preferred_element_type=F32)
        key_sum[...] += jnp.dot(score_grad, query_low_ref[:, span], preferred_element_type=F32)
        turned = jnp.dot(key_turned_ref[...], score_grad, preferred_element_type=F32)
        query_back = (turned.T * scale).astype(BF).astype(F32)
        grad, gain = norm_parts(
            query_raw_ref[:, span], query_gain_ref[...], turn_back(query_back, cos, sin)
        )
        gains_ref[0:1, :] += gain
        start = pl.multiple_of(step * cols + head * head_dim, head_dim)
        grads_ref[:, pl.ds(start, head_dim)] = grad.astype(BF)

    @pl.when(step == pl.num_programs(0) - 1)
    def _():
        key_back = (key_sum[...] * scale).astype(BF).astype(F32)
        grad, gain = norm_parts(key_raw_ref[...], key_gain_ref[...], turn_back(key_back, cos, sin))
        gains_ref[1:2, :] += gain
        last = grads_ref.shape[1]
        grads_ref[:, last - 2 * head_dim : last - head_dim] = grad.astype(BF)
        grads_ref[:, last - head_dim :] = value_sum[...].astype(BF)


def attend_back(
    blocks, output_weight, query_raw, query_low, probs, key_raw, key_low, value_low, cos, sin, query_gain, key_gain, weight=0.1
):
    count, (size, wide), width = len(blocks), blocks[0].shape, output_weight.shape[0]
    length, cols = query_raw.shape
    head_dim = query_gain.shape[0]
    step = min(2 * head_dim, cols)
    single = fixed((length, head_dim))
    narrow = pl.BlockSpec((length, step), lambda i: (0, i))
    return pl.pallas_call(
        lambda *refs: attend_back_kernel(count, head_dim, 1.0 / math.sqrt(head_dim), *refs),
        grid=(cols // step,),
        in_specs=[fixed((size, wide))] * count
        + [
            pl.BlockSpec((width, step), lambda i: (0, i)), narrow, narrow,
            pl.BlockSpec((step // head_dim, length, length), lambda i: (i, 0, 0)),
            single, single, single, single, single, fixed((1, head_dim)), fixed((1, head_dim)),
        ],
        out_specs=[
            fixed((length, width)), fixed((length, wide - width)),
            fixed((length, cols + 2 * head_dim)), fixed((8, head_dim)),
        ],
        out_shape=[
            jax.ShapeDtypeStruct((length, width), BF),
            jax.ShapeDtypeStruct((length, wide - width), BF),
            jax.ShapeDtypeStruct((length, cols + 2 * head_dim), BF),
            jax.ShapeDtypeStruct((8, head_dim), F32),
        ],
        scratch_shapes=[
            pltpu.VMEM((head_dim, length), BF),
            pltpu.VMEM((length, head_dim), F32),
            pltpu.VMEM((length, head_dim), F32),
        ],
        compiler_params=params(),
        cost_estimate=cost(2 * length * width * cols, 2 * width * cols, weight),
    )(
        *blocks, output_weight, query_raw, query_low, probs, key_raw, key_low, value_low, cos, sin,
        query_gain[None, :], key_gain[None, :],
    )


def route_kernel(
    capacity, tp_count,
    routes_ref, turned_ref, rows_ref,
    mask_ref, turned_mask_ref, routed_ref, sent_ref,
    places_ref,
):
    length, top_count = routes_ref.shape
    experts, slots = routed_ref.shape[1], mask_ref.shape[1]
    owners = slots // capacity
    step, tile = pl.program_id(0), turned_mask_ref.shape[0]
    me = lax.axis_index("tp")

    def iota(shape, axis):
        return lax.broadcasted_iota(jnp.int32, shape, axis)

    def low(flags):
        return flags.astype(F32).astype(BF)

    @pl.when(step == 0)
    def _():
        expert = iota((length, experts), 1)
        routed = jnp.zeros((length, experts), F32)
        turned = jnp.zeros((experts, length), F32)
        for k in range(top_count):
            routed += (routes_ref[:, k : k + 1] == expert).astype(F32)
            turned += (turned_ref[k : k + 1, :] == iota((experts, length), 0)).astype(F32)
        routed_ref[...] = routed.astype(BF)
        own = jnp.dot(
            routed_ref[...],
            low(iota((experts, owners), 0) == iota((experts, owners), 1) * tp_count + me),
            preferred_element_type=F32,
        )
        earlier = low(iota((length, length), 0) > iota((length, length), 1))
        rank = jnp.dot(earlier, own.astype(BF), preferred_element_type=F32)
        places = jnp.where(own > 0.5, rank, -1.0).astype(BF)
        slot = iota((owners, slots), 1)
        wide = jnp.dot(
            places, low(lax.div(slot, capacity) == iota((owners, slots), 0)), preferred_element_type=F32
        )
        mask_ref[...] = low(wide == lax.rem(iota((1, slots), 1), capacity).astype(F32))
        own_turned = jnp.dot(
            low(iota((owners, experts), 1) == iota((owners, experts), 0) * tp_count + me),
            turned.astype(BF),
            preferred_element_type=F32,
        )
        later = low(iota((length, length), 0) < iota((length, length), 1))
        rank_turned = jnp.dot(own_turned.astype(BF), later, preferred_element_type=F32)
        places_ref[...] = jnp.where(own_turned > 0.5, rank_turned, -1.0).astype(BF)

    slot = iota((tile, owners), 0) + step * tile
    wide = jnp.dot(
        low(lax.div(slot, capacity) == iota((tile, owners), 1)), places_ref[...], preferred_element_type=F32
    )
    mask = low(wide == lax.rem(iota((tile, 1), 0) + step * tile, capacity).astype(F32))
    turned_mask_ref[...] = mask
    width = rows_ref.shape[1]
    sent_ref[:, :width] = jnp.dot(mask, rows_ref[...], preferred_element_type=F32).astype(BF)
    sent_ref[:, width:] = jnp.dot(mask, routed_ref[...], preferred_element_type=F32).astype(BF)


def route(routes, rows, experts, capacity, ep_count, tp_count, weight=1.0):
    (length, top_count), width = routes.shape, rows.shape[1]
    slots = ep_count * capacity
    tile = min(256, slots)
    return pl.pallas_call(
        lambda *refs: route_kernel(capacity, tp_count, *refs),
        grid=(slots // tile,),
        in_specs=[fixed((length, top_count)), fixed((top_count, length)), fixed((length, width))],
        out_specs=[
            fixed((length, slots)),
            pl.BlockSpec((tile, length), lambda i: (i, 0)),
            fixed((length, experts)),
            pl.BlockSpec((tile, width + experts), lambda i: (i, 0)),
        ],
        out_shape=[
            jax.ShapeDtypeStruct((length, slots), BF),
            jax.ShapeDtypeStruct((slots, length), BF),
            jax.ShapeDtypeStruct((length, experts), BF),
            pltpu.HBM((slots, width + experts), BF),
        ],
        scratch_shapes=[pltpu.VMEM((ep_count, length), BF)],
        compiler_params=params(),
        cost_estimate=cost(2 * length * slots * width, 2 * slots * width, weight),
    )(routes, routes.T, rows)


def gate_kernel(capacity, tp_count, rows_ref, router_ref, routed_ref, mask_ref, probs_ref, weight_ref):
    experts, slots = routed_ref.shape[1], mask_ref.shape[1]
    owners = slots // capacity
    me = lax.axis_index("tp")

    def iota(shape, axis):
        return lax.broadcasted_iota(jnp.int32, shape, axis)

    logits = jnp.dot(rows_ref[...], router_ref[...], preferred_element_type=F32)
    logits = jnp.where(routed_ref[...].astype(F32) > 0.5, logits, MASKED)
    exps = jnp.exp(logits - jnp.max(logits, axis=1, keepdims=True))
    probs = exps / jnp.sum(exps, axis=1, keepdims=True)
    probs_ref[...] = probs
    spread = (
        iota((experts, slots), 0) == lax.div(iota((experts, slots), 1), capacity) * tp_count + me
    )
    weights = jnp.dot(
        probs.astype(BF), spread.astype(F32).astype(BF), preferred_element_type=F32
    )
    weight_ref[...] = weights.astype(BF) * mask_ref[...]


def gate_weights(rows, router_weight, routed, mask, capacity, ep_count, tp_count, weight=1.0):
    length, slots = mask.shape
    return pl.pallas_call(
        lambda *refs: gate_kernel(capacity, tp_count, *refs),
        out_shape=[
            jax.ShapeDtypeStruct(routed.shape, F32),
            jax.ShapeDtypeStruct((length, slots), BF),
        ],
        compiler_params=params(),
        cost_estimate=cost(2 * length * routed.shape[1] * (rows.shape[1] + slots), 4 * length * slots, weight),
    )(rows, router_weight, routed, mask)


def fill_kernel(count, *refs):
    blocks, (mask_ref, sent_ref, whole_ref) = refs[:count], refs[count:]

    @pl.when(pl.program_id(0) == 0)
    def _():
        gather_rows(blocks, whole_ref)

    sent_ref[...] = jnp.dot(mask_ref[...], whole_ref[...], preferred_element_type=F32).astype(BF)


def fill(blocks, turned_mask, weight=0.1):
    count, (size, width) = len(blocks), blocks[0].shape
    slots, length = turned_mask.shape
    tile = min(256, slots)
    return pl.pallas_call(
        lambda *refs: fill_kernel(count, *refs),
        grid=(slots // tile,),
        in_specs=[fixed((size, width))] * count + [pl.BlockSpec((tile, length), lambda i: (i, 0))],
        out_specs=[pl.BlockSpec((tile, width), lambda i: (i, 0)), fixed((length, width))],
        out_shape=[
            pltpu.HBM((slots, width), BF),
            jax.ShapeDtypeStruct((length, width), BF),
        ],
        compiler_params=params(),
        cost_estimate=cost(2 * length * slots * width, 2 * slots * width, weight),
    )(*blocks, turned_mask)


def after(value, *earlier):
    return lax.optimization_barrier((value,) + earlier)[0]


def ring(count, shift):
    return [(i, (i + shift) % count) for i in range(count)]


def row_block(value_rows, index, count):
    size = value_rows.shape[0] // count
    return lax.dynamic_slice_in_dim(value_rows, index * size, size, 0)


def tp_spread(block):
    count = lax.axis_size("tp")
    return [block] + [lax.ppermute(block, "tp", ring(count, shift)) for shift in range(1, count)]


def tp_join(blocks):
    count, me = lax.axis_size("tp"), lax.axis_index("tp")
    whole = jnp.zeros((count,) + blocks[0].shape, blocks[0].dtype)
    for shift, block in enumerate(blocks):
        whole = lax.dynamic_update_index_in_dim(whole, block, (me - shift) % count, 0)
    return whole.reshape((-1,) + blocks[0].shape[1:])


def tp_sum_blocks(blocks):
    count = lax.axis_size("tp")
    total = blocks[0].astype(F32)
    for shift in range(1, count):
        total = total + lax.ppermute(blocks[shift], "tp", ring(count, shift)).astype(F32)
    return total


def project_kernel(count, spans, left_ref, *refs):
    rights, refs = refs[: len(spans)], refs[len(spans) :]
    outs, held = refs[-count - 1 : -1], refs[-1]
    me = lax.axis_index("tp")
    size = left_ref.shape[0] // count
    for right_ref, (first, last) in zip(rights, spans):
        got = lax.dot_general(
            left_ref[:, first:last], right_ref[...], COLS, preferred_element_type=F32
        )
        if first == 0:
            held[...] = got
        else:
            held[...] += got
    for shift in range(count):
        start = pl.multiple_of((me + shift) % count * size, size)
        outs[shift][...] = held[pl.ds(start, size), :].astype(BF)
    if len(refs) > count + 1:
        rows_ref, rate_ref, gain_ref = refs[:3]
        gain_ref[...] = jnp.sum(
            held[...] * (rows_ref[...].astype(F32) * rate_ref[:, :1]), axis=0, keepdims=True
        )


def project(left, rights, rows=None, rate=None, tile=512, weight=1.0):
    count = lax.axis_size("tp")
    length, width = left.shape[0], rights[0].shape[0]
    tile = min(tile, width)
    spans, first = [], 0
    for right in rights:
        spans.append((first, first + right.shape[1]))
        first += right.shape[1]
    size = length // count
    in_specs = [fixed(left.shape)]
    in_specs += [pl.BlockSpec((tile, right.shape[1]), lambda i: (i, 0)) for right in rights]
    out_specs = [pl.BlockSpec((size, tile), lambda i: (0, i))] * count
    out_shape = [jax.ShapeDtypeStruct((size, width), BF)] * count
    more = []
    if rows is not None:
        more = [rows, rate]
        in_specs += [pl.BlockSpec((length, tile), lambda i: (0, i)), fixed(rate.shape)]
        out_specs = [pl.BlockSpec((1, tile), lambda i: (0, i))] + out_specs
        out_shape = [jax.ShapeDtypeStruct((1, width), F32)] + out_shape
    return pl.pallas_call(
        lambda *refs: project_kernel(count, spans, *refs),
        grid=(width // tile,),
        in_specs=in_specs,
        out_specs=out_specs,
        out_shape=out_shape,
        scratch_shapes=[pltpu.VMEM((length, tile), F32)],
        compiler_params=params(),
        cost_estimate=cost(2 * length * first * width, 2 * first * width, weight),
    )(left, *rights, *more)


def expert_kernel(
    width, rows_ref, grads_ref, *refs
):
    count = (len(refs) - 7) // 2
    sources = [refs[:count], refs[count : 2 * count]]
    back_ref, act_ref, gate_back_ref, up_back_ref, *held, sems = refs[2 * count :]
    size = sources[0][0].shape[0]

    def loads(which):
        return [
            pltpu.make_async_copy(
                source, held[which].at[pl.ds(part * size, size), :], sems.at[which, part]
            )
            for part, source in enumerate(sources[which])
        ]

    first = pl.program_id(0) == 0

    @pl.when(first)
    def _():
        for which in range(2):
            for load in loads(which):
                load.start()
        for load in loads(0):
            load.wait()

    rows = rows_ref[...]
    gate_val = lax.dot_general(rows, held[0][...], COLS, preferred_element_type=F32)

    @pl.when(first)
    def _():
        for load in loads(1):
            load.wait()

    up_val = lax.dot_general(rows, held[1][...], COLS, preferred_element_type=F32)

    act_grad = grads_ref[...]
    gate_sig = jax.nn.sigmoid(gate_val)
    gate_act = gate_val * gate_sig
    act_low = (gate_act * up_val).astype(BF)
    act_ref[...] = act_low
    gate_back = (act_grad * up_val * gate_sig * (1.0 + gate_val * (1.0 - gate_sig))).astype(BF)
    up_back = (act_grad * gate_act).astype(BF)
    gate_back_ref[...] = gate_back
    up_back_ref[...] = up_back
    slot_grad = jnp.sum(act_low.astype(F32) * act_grad, axis=1, keepdims=True)
    back_ref[:, width:] = jnp.broadcast_to(
        slot_grad, (rows.shape[0], back_ref.shape[1] - width)
    ).astype(BF)
    back_ref[:, :width] = (
        jnp.dot(gate_back, held[0][...], preferred_element_type=F32)
        + jnp.dot(up_back, held[1][...], preferred_element_type=F32)
    ).astype(BF)


def hidden_kernel(rows_ref, *refs):
    blocks, out_ref = refs[:-1], refs[-1]
    size = blocks[0].shape[0]
    for part, block in enumerate(blocks):
        out_ref[:, part * size : (part + 1) * size] = lax.dot_general(
            rows_ref[...], block[...], COLS, preferred_element_type=F32
        )


def hidden_grads(rows, downs, tile=256, weight=10.0):
    slots, (size, width) = rows.shape[0], downs[0].shape
    tile = min(tile, slots)
    return pl.pallas_call(
        hidden_kernel,
        grid=(slots // tile,),
        in_specs=[pl.BlockSpec((tile, width), lambda i: (i, 0))] + [fixed((size, width))] * len(downs),
        out_specs=pl.BlockSpec((tile, size * len(downs)), lambda i: (i, 0)),
        out_shape=pltpu.HBM((slots, size * len(downs)), F32),
        compiler_params=params(),
        cost_estimate=cost(2 * slots * width * size * len(downs), 2 * slots * width, weight),
    )(rows, *downs)


def expert_pass(rows_in, act_grad, gates, ups, extra, tile=256, weight=1.0):
    slots, width = rows_in.shape
    tile = min(tile, slots)
    hidden = len(gates) * gates[0].shape[0]
    tall = pl.BlockSpec((tile, width), lambda i: (i, 0))
    narrow = pl.BlockSpec((tile, hidden), lambda i: (i, 0))
    low = jax.ShapeDtypeStruct((slots, hidden), BF)
    return pl.pallas_call(
        lambda *refs: expert_kernel(width, *refs),
        grid=(slots // tile,),
        in_specs=[tall, narrow] + [pl.BlockSpec(memory_space=pl.ANY)] * (2 * len(gates)),
        out_specs=[pl.BlockSpec((tile, width + extra), lambda i: (i, 0)), narrow, narrow, narrow],
        out_shape=[pltpu.HBM((slots, width + extra), BF), low, low, low],
        scratch_shapes=[pltpu.VMEM((hidden, width), BF)] * 2
        + [pltpu.SemaphoreType.DMA((2, len(gates)))],
        compiler_params=params(),
        cost_estimate=cost(8 * slots * width * hidden, 6 * slots * width + 6 * width * hidden, weight),
    )(rows_in, act_grad, *gates, *ups)


def place_kernel(count, *refs):
    ins, out_ref = refs[:count], refs[count]
    step = pl.program_id(0)
    for shift in range(count):

        @pl.when(step == shift)
        def _():
            out_ref[0] = ins[shift][...].astype(out_ref.dtype)


def place_blocks(blocks, direction, dtype, tile, weight=1.0):
    count, me = len(blocks), lax.axis_index("tp")
    rows, cols = blocks[0].shape
    steps = rows // tile

    def held(shift):
        return lambda s, t, me_ref: (jnp.where(s < shift, 0, jnp.where(s > shift, steps - 1, t)), 0)

    return pl.pallas_call(
        lambda me_ref, *refs: place_kernel(count, *refs),
        grid_spec=pltpu.PrefetchScalarGridSpec(
            num_scalar_prefetch=1,
            grid=(count, steps),
            in_specs=[pl.BlockSpec((tile, cols), held(shift)) for shift in range(count)],
            out_specs=pl.BlockSpec(
                (1, tile, cols), lambda s, t, me_ref: ((me_ref[0] + direction * s + count) % count, t, 0)
            ),
        ),
        out_shape=jax.ShapeDtypeStruct((count, rows, cols), dtype),
        compiler_params=params(),
        cost_estimate=cost(0, count * rows * cols * (2 + jnp.dtype(dtype).itemsize), weight),
    )(me.astype(jnp.int32).reshape(1), *blocks)


def pull_slices(weights, picks):
    count, me = lax.axis_size("tp"), lax.axis_index("tp")
    return [
        lax.dynamic_index_in_dim(weights[which], (me + shift) % count, 0, keepdims=False)
        for which, shift in picks
    ]


def shift_blocks(blocks, shifts):
    count = lax.axis_size("tp")
    return [
        lax.ppermute(block, "tp", ring(count, shift)) for block, shift in zip(blocks, shifts)
    ]


def push_blocks(grad, shifts=None):
    count = lax.axis_size("tp")
    size = grad.shape[0] // count
    blocks = []
    for shift in range(count) if shifts is None else shifts:
        block = grad[shift * size : (shift + 1) * size]
        blocks.append(lax.ppermute(block, "tp", ring(count, -shift)) if shift else block)
    return blocks


def place_experts(blocks):
    return place_blocks(blocks, 1, F32, blocks[0].shape[0])


def ep_exchange(rows):
    return lax.all_to_all(rows, "ep", 0, 0, tiled=True)


def wgrad_kernel(share, spans, *refs):
    count = len(spans)
    lefts, rights, (keep_ref, send_ref, held) = refs[:count], refs[count : 2 * count], refs[2 * count :]
    core = lax.axis_index("ep") % 2
    for left_ref, right_ref, (first, size) in zip(lefts, rights, spans):
        held[:, first : first + size] = lax.dot_general(
            left_ref[...], right_ref[...], ROWS, preferred_element_type=F32
        )
    split_cores(share, core, held, keep_ref, send_ref)


def split_cores(share, core, held, keep_ref, send_ref):
    for chip in range(held.shape[0] // (2 * share)):
        kept = pl.multiple_of((2 * chip + core) * share, share)
        sent = pl.multiple_of((2 * chip + 1 - core) * share, share)
        keep_ref[chip * share : (chip + 1) * share, :] = held[pl.ds(kept, share), :].astype(BF)
        send_ref[chip * share : (chip + 1) * share, :] = held[pl.ds(sent, share), :].astype(BF)


def grad_halves(pairs, tile=512, weight=1.0):
    count = lax.axis_size("ep")
    length, width = pairs[0][0].shape
    share = width // count
    tile = min(tile, width)
    spans, cols = [], 0
    for _, right in pairs:
        spans.append((cols, right.shape[1]))
        cols += right.shape[1]
    half = pl.BlockSpec((tile // 2, cols), lambda i: (i, 0))
    return pl.pallas_call(
        lambda *refs: wgrad_kernel(share, spans, *refs),
        grid=(width // tile,),
        in_specs=[pl.BlockSpec((length, tile), lambda i: (0, i))] * len(pairs)
        + [pl.BlockSpec(right.shape, lambda i: (0, 0)) for _, right in pairs],
        out_specs=[half, half],
        out_shape=[pltpu.HBM((width // 2, cols), BF)] * 2,
        scratch_shapes=[pltpu.VMEM((tile, cols), F32)],
        compiler_params=params(),
        cost_estimate=cost(2 * length * width * cols, 3 * width * cols, weight),
    )(*[left for left, _ in pairs], *[right for _, right in pairs])


def swap_cores(value):
    return lax.ppermute(value, "ep", [(i, i ^ 1) for i in range(lax.axis_size("ep"))])


def pair_kernel(share, first_keep, first_got, second_keep, second_got, extra_ref, out_ref):
    for chip in range(out_ref.shape[0]):
        rows, row = slice(chip * share, (chip + 1) * share), 0
        for keep_ref, got_ref in ((first_keep, first_got), (second_keep, second_got)):
            for column in range(0, keep_ref.shape[1], 128):
                span = slice(column, column + 128)
                both = keep_ref[rows, span].astype(F32) + got_ref[rows, span].astype(F32)
                out_ref[chip, row : row + share, :] = both.astype(BF)
                row += share
        out_ref[chip, row:, :] = extra_ref[chip]


def pair_sums(pairs, extra, weight=1.0):
    chips = extra.shape[0]
    share = pairs[0][0].shape[0] // chips
    step = min(4, chips)
    blocks = [pl.BlockSpec((step * share, keep.shape[1]), lambda i: (i, 0)) for keep, _ in pairs for _ in range(2)]
    rows = sum(keep.shape[1] // 128 * share for keep, _ in pairs) + extra.shape[1]
    return pl.pallas_call(
        lambda *refs: pair_kernel(share, *refs),
        grid=(chips // step,),
        in_specs=blocks + [pl.BlockSpec((step,) + extra.shape[1:], lambda i: (i, 0, 0))],
        out_specs=pl.BlockSpec((step, rows, 128), lambda i: (i, 0, 0)),
        out_shape=pltpu.HBM((chips, rows, 128), BF),
        compiler_params=params(),
        cost_estimate=cost(0, 8 * chips * rows * 128, weight),
    )(*[value for pair in pairs for value in pair], extra)


def chip_kernel(widths, parts_ref, *outs):
    share, row = outs[0].shape[0], 0
    for out_ref, width in zip(outs, widths):
        for column in range(0, width, 128):
            part = parts_ref[:, row : row + share, :].astype(F32)
            out_ref[:, column : column + 128] = jnp.sum(part, axis=0)
            row += share
    outs[-1][...] = jnp.sum(parts_ref[:, row:, :].astype(F32), axis=0)


def chip_sums(parts, widths, share, weight=1.0):
    rest = parts.shape[1] - sum(widths) // 128 * share
    return pl.pallas_call(
        lambda *refs: chip_kernel(widths, *refs),
        out_shape=[jax.ShapeDtypeStruct((share, width), F32) for width in widths]
        + [jax.ShapeDtypeStruct((rest, 128), F32)],
        compiler_params=params(),
        cost_estimate=cost(0, 2 * parts.size, weight),
    )(parts)


def chip_exchange(parts):
    count = lax.axis_size("ep")
    if count == 2:
        return parts
    groups = [list(range(side, count, 2)) for side in range(2)]
    return lax.all_to_all(parts, "ep", 0, 0, axis_index_groups=groups, tiled=True)


def core_sum(extra):
    core, many = lax.axis_index("ep") % 2, extra.shape[1]
    extra = extra.reshape(-1, 2, many)
    total = lax.dynamic_index_in_dim(extra, core, 1, keepdims=False)
    total += swap_cores(lax.dynamic_index_in_dim(extra, 1 - core, 1, keepdims=False))
    total = total.reshape(total.shape[0], -1, 128)
    high = total.astype(BF)
    low = (total - high.astype(F32)).astype(BF)
    rows = jnp.concatenate([high, low], axis=1)
    return jnp.pad(rows, ((0, 0), (0, -rows.shape[1] % 8), (0, 0)))


def combine_kernel(count, capacity, width, weight_ref, mask_ref, rows_ref, *refs):
    outs, held = refs[:-1], refs[-1]
    me = lax.axis_index("tp")
    size = weight_ref.shape[0] // count
    shape = (rows_ref.shape[0], rows_ref.shape[1] - width)
    owner = lax.div(lax.broadcasted_iota(jnp.int32, shape, 0), capacity)
    named = owner * count + me == lax.broadcasted_iota(jnp.int32, shape, 1)
    held[:, :width] = jnp.dot(weight_ref[...], rows_ref[:, :width], preferred_element_type=F32)
    held[:, width:] = jnp.dot(
        mask_ref[...], rows_ref[:, width:] * named.astype(F32).astype(BF), preferred_element_type=F32
    )
    for shift in range(count):
        start = pl.multiple_of((me + shift) % count * size, size)
        outs[shift][...] = held[pl.ds(start, size), :].astype(BF)


def combine(weights, mask, rows, width, capacity, weight=0.0):
    count = lax.axis_size("tp")
    length, wide = weights.shape[0], rows.shape[1]
    return pl.pallas_call(
        lambda *refs: combine_kernel(count, capacity, width, *refs),
        out_shape=[jax.ShapeDtypeStruct((length // count, wide), BF)] * count,
        scratch_shapes=[pltpu.VMEM((length, wide), F32)],
        compiler_params=params(),
        cost_estimate=cost(2 * length * rows.shape[0] * wide, 2 * rows.shape[0] * wide, weight),
    )(weights, mask, rows)


def mix_kernel(count, weight_ref, rows_ref, *refs):
    outs, held = refs[:-1], refs[-1]
    me = lax.axis_index("tp")
    size = weight_ref.shape[0] // count
    held[...] = jnp.dot(weight_ref[...], rows_ref[...], preferred_element_type=F32)
    for shift in range(count):
        start = pl.multiple_of((me + shift) % count * size, size)
        outs[shift][...] = held[pl.ds(start, size), :].astype(BF)


def mix(weights, rows, tile=512, weight=10.0):
    count = lax.axis_size("tp")
    (length, slots), width = weights.shape, rows.shape[1]
    tile = min(tile, width)
    return pl.pallas_call(
        lambda *refs: mix_kernel(count, *refs),
        grid=(width // tile,),
        in_specs=[fixed((length, slots)), pl.BlockSpec((slots, tile), lambda i: (0, i))],
        out_specs=[pl.BlockSpec((length // count, tile), lambda i: (0, i))] * count,
        out_shape=[jax.ShapeDtypeStruct((length // count, width), BF)] * count,
        scratch_shapes=[pltpu.VMEM((length, tile), F32)],
        compiler_params=params(),
        cost_estimate=cost(2 * length * slots * width, 2 * slots * width, weight),
    )(weights, rows)


def tp_sum(value):
    count, total = lax.axis_size("tp"), value
    for shift in range(1, count):
        total = total + lax.ppermute(value, "tp", ring(count, shift))
    return total


def per_device(
    tokens,
    doc_ids,
    routes,
    query_weight,
    key_matrix,
    value_matrix,
    output_weight,
    attn_gain,
    query_gain,
    key_gain,
    mlp_gain,
    router_weight,
    gate_weight,
    up_weight,
    down_weight,
    cotangent,
):
    length, width = tokens.shape
    head_dim = query_gain.shape[0]
    total_experts = router_weight.shape[1]
    top_count = routes.shape[1]
    ep_count, tp_count = lax.axis_size("ep"), lax.axis_size("tp")
    ep_index, tp_index = lax.axis_index("ep"), lax.axis_index("tp")
    capacity = length * top_count * 4 // (3 * total_experts)
    slots = ep_count * capacity

    near, far = (1, tp_count - 1), range(2, tp_count - 1)
    weights = (jnp.swapaxes(gate_weight, 1, 2), jnp.swapaxes(up_weight, 1, 2), down_weight)
    near_gates_out = pull_slices(weights, [(0, shift) for shift in near])
    far_gates_out = pull_slices(weights, [(0, shift) for shift in far])
    near_ups_out = pull_slices(weights, [(1, shift) for shift in near])
    far_ups_out = pull_slices(weights, [(1, shift) for shift in far])
    near_downs_out = pull_slices(weights, [(2, shift) for shift in near])
    far_downs_out = pull_slices(weights, [(2, shift) for shift in far])
    (tokens,), near_gates_out, far_gates_out = joined((tokens,), near_gates_out, far_gates_out)
    (tokens,), near_gates_out = joined((tokens,), near_gates_out)
    near_gates = shift_blocks(near_gates_out, near)

    def dispatch(sent):
        return ep_exchange(sent.reshape(ep_count, capacity, -1)).reshape(slots, -1)

    (tokens,), = joined((tokens,))
    (tokens,), = joined((tokens,))
    cos, sin = rope_tables(doc_ids, head_dim)
    (
        first_normed, rate_first, heads_low, query_raw, query_low, probs, key_raw, key_low, value_low,
    ) = attend(
        tokens, doc_ids, query_weight, key_matrix, value_matrix, attn_gain, query_gain, key_gain, cos, sin
    )

    (cotangent, heads_low), = joined((cotangent, heads_low))
    (cotangent,), near_gates = joined((cotangent,), near_gates)
    (cotangent,), far_gates_out = joined((cotangent,), far_gates_out)
    far_gates = shift_blocks(far_gates_out, far)
    send_mask, turned_mask, routed, sent_grads = route(
        routes, cotangent, total_experts, capacity, ep_count, tp_count
    )
    (heads_low, sent_grads), = joined((heads_low, sent_grads))
    (sent_grads,), = joined((sent_grads,))
    (sent_grads,), = joined((sent_grads,))
    (heads_low,), far_gates = joined((heads_low,), far_gates)
    (heads_low,), = joined((heads_low,))
    attn_parts = project(heads_low, [output_weight], weight=PROJECT_FIRST)
    grads_in = dispatch(sent_grads)

    tokens_own = row_block(tokens, tp_index, tp_count).astype(F32)
    upstream_own = row_block(cotangent, tp_index, tp_count).astype(F32)
    hidden = tokens_own + tp_sum_blocks(attn_parts)
    rate_second = norm_rate(hidden)
    normed_own = (hidden * rate_second * mlp_gain).astype(BF)
    own = pull_slices(weights, [(0, 0), (1, 0), (2, 0)])
    (normed_own,), near_ups_out, far_ups_out, near_downs_out, far_downs_out = joined((normed_own,), near_ups_out, far_ups_out, near_downs_out, far_downs_out)
    (normed_own,), = joined((normed_own,))
    (normed_own,), near_ups_out, far_ups_out, near_downs_out = joined((normed_own,), near_ups_out, far_ups_out, near_downs_out)
    near_ups = shift_blocks(near_ups_out, near)
    far_ups = shift_blocks(far_ups_out, far)
    near_downs = shift_blocks(near_downs_out, near)
    normed_blocks = tp_spread(normed_own)
    normed_blocks, far_downs_out = joined(normed_blocks, far_downs_out)
    far_downs = shift_blocks(far_downs_out, far)
    normed_blocks, = joined(normed_blocks)
    sent_rows, normed_second = fill(normed_blocks, turned_mask)
    rows_in = dispatch(sent_rows)
    (normed_second,), far_downs = joined((normed_second,), far_downs)

    columns = jnp.arange(total_experts, dtype=jnp.int32)
    slot_logits = jnp.dot(rows_in, router_weight, preferred_element_type=F32)
    slot_logits = jnp.where(grads_in[:, width:].astype(F32) > 0.5, slot_logits, MASKED)
    slot_exp = jnp.exp(slot_logits - jnp.max(slot_logits, axis=-1, keepdims=True))
    own_expert = (columns == ep_index * tp_count + tp_index).astype(F32)
    probs_in = jnp.sum(slot_exp * own_expert[None, :], axis=-1) / jnp.sum(slot_exp, axis=-1)

    (grads_in,), near_downs = joined((grads_in,), near_downs)
    downs = [own[2], near_downs[0], *far_downs, near_downs[1]]
    down_full = jnp.concatenate(downs, axis=0)
    act_grad = hidden_grads(grads_in, downs)
    (act_grad,), near_ups, far_ups = joined((act_grad,), near_ups, far_ups)
    gates = [own[0], near_gates[0], *far_gates, near_gates[1]]
    ups = [own[1], near_ups[0], *far_ups, near_ups[1]]
    rows_grad, act_low, gate_back, up_back = expert_pass(rows_in, act_grad, gates, ups, total_experts)
    (normed_second, act_low), = joined((normed_second, act_low))
    gate_probs, weigh_back = gate_weights(
        normed_second, router_weight, routed, send_mask, capacity, ep_count, tp_count
    )
    back_rows = dispatch(rows_grad)
    expert_out = jnp.dot(act_low, down_full, preferred_element_type=F32).astype(BF)

    def expert_grad(left, right):
        weighed = (left.astype(F32) * probs_in[:, None]).astype(BF)
        return lax.dot_general(weighed, right, ROWS, preferred_element_type=F32).astype(BF)

    down_blocks = push_blocks(expert_grad(act_low, grads_in[:, :width]))
    gate_part = expert_grad(gate_back, rows_in)
    up_part = expert_grad(up_back, rows_in)
    unit = gate_part.shape[0] // tp_count

    def part_of(part, shift):
        return part[shift * unit : (shift + 1) * unit]

    own_parts = [part_of(gate_part, 0), part_of(up_part, 0)]
    gate_near = [part_of(gate_part, shift) for shift in near]
    up_near = [part_of(up_part, shift) for shift in near]
    far_parts = [
        jnp.concatenate([part_of(gate_part, shift), part_of(up_part, shift)], axis=0) for shift in far
    ]
    back_near, back_far = [-shift for shift in near], [-shift for shift in far]
    down_group = [place_experts(down_blocks)]
    pushed_gates = shift_blocks(gate_near, back_near)
    held = (back_rows, expert_out, *down_group)
    held, pushed_gates, own_parts, up_near, far_parts = joined(held, pushed_gates, own_parts, up_near, far_parts)
    back_rows, expert_out, *down_group = held

    input_parts = combine(weigh_back, send_mask, back_rows, width, capacity)
    (down_wgrad,) = down_group
    expert_out, *input_parts = joined((expert_out, *input_parts))[0]
    returned = [dispatch(expert_out)]
    back_sum = tp_sum_blocks(input_parts)

    gate_grad = back_sum[:, width:]
    probs_own = row_block(gate_probs, tp_index, tp_count)
    gate_mean = jnp.sum(probs_own * gate_grad, axis=-1, keepdims=True)
    logit_own = (probs_own * (gate_grad - gate_mean)).astype(BF)
    router_input = lax.dot_general(logit_own, router_weight, COLS, preferred_element_type=F32)
    second_grad = router_input + back_sum[:, :width]
    mlp_gain_part = jnp.sum(second_grad * hidden * rate_second, axis=0)
    hidden_grad = upstream_own + norm_back(hidden, rate_second, mlp_gain, second_grad)
    branch_blocks = tp_spread(jnp.concatenate([hidden_grad.astype(BF), logit_own], axis=1))
    branch_blocks, up_near = joined(branch_blocks, up_near)
    pushed_ups = shift_blocks(up_near, back_near)
    branch_blocks, = joined(branch_blocks)

    branch_low, logit_grad, raw_grads, head_gains = attend_back(
        branch_blocks, output_weight, query_raw, query_low, probs, key_raw, key_low, value_low, cos, sin, query_gain, key_gain
    )
    (branch_low, raw_grads), = joined((branch_low, raw_grads))
    (raw_grads,), pushed_ups = joined((raw_grads,), pushed_ups)
    attn_gain_part, *first_parts = project(
        raw_grads, [query_weight, key_matrix, value_matrix], tokens, rate_first, weight=PROJECT_LAST
    )
    share = width // ep_count
    gains = jnp.concatenate(
        [
            attn_gain_part.reshape(ep_count, share),
            mlp_gain_part.reshape(ep_count, share),
            jnp.broadcast_to(head_gains[:2].reshape(1, -1), (ep_count, 2 * head_dim)),
        ],
        axis=1,
    )
    raw_keep, raw_send = grad_halves([(first_normed, raw_grads)], weight=HALVES_FIRST)
    raw_got = swap_cores(raw_send)
    extra = core_sum(gains)
    first_grad = tp_sum_blocks(first_parts)
    (first_grad,), returned = joined((first_grad,), returned)
    (first_grad, branch_low), = joined((first_grad, branch_low))
    (branch_low,), = joined((branch_low,))
    logits_wide = jnp.pad(logit_grad, ((0, 0), (0, -total_experts % 128)))
    later_pair = grad_halves([(branch_low, heads_low), (normed_second, logits_wide)], weight=HALVES_LATER)
    later_pair = (later_pair[0], swap_cores(later_pair[1]))
    (first_grad,), far_parts = joined((first_grad,), far_parts)
    pushed_far = shift_blocks(far_parts, back_far)
    sums = pair_sums([(raw_keep, raw_got), later_pair], extra)
    rate_own = row_block(rate_first, tp_index, tp_count)[:, :1]
    (first_grad, sums), = joined((first_grad, sums))
    tokens_own_grad = hidden_grad + norm_back(tokens_own, rate_own, attn_gain, first_grad)
    token_blocks = tp_spread(tokens_own_grad.astype(BF))
    token_blocks, = joined(token_blocks)
    tokens_grad = tp_join(token_blocks)

    returned, = joined(returned)
    layer_own = (hidden + tp_sum_blocks(mix(weigh_back, returned[0]))).astype(BF)
    (layer_own,), = joined((layer_own,))

    widths = (
        query_weight.shape[1], key_matrix.shape[1], value_matrix.shape[1], heads_low.shape[1], total_experts + -total_experts % 128,
    )
    query_wgrad, key_wgrad, value_wgrad, output_wgrad, router_wgrad, gain_rows = chip_sums(
        chip_exchange(sums), widths, share
    )
    many = gains.shape[1] // 128
    gain_total = tp_sum((gain_rows[:many] + gain_rows[many : 2 * many]).reshape(-1))
    layer_blocks = tp_spread(layer_own)
    gate_blocks = [own_parts[0], pushed_gates[0], *[block[:unit] for block in pushed_far], pushed_gates[1]]
    up_blocks = [own_parts[1], pushed_ups[0], *[block[unit:] for block in pushed_far], pushed_ups[1]]
    layer_out = tp_join(layer_blocks)
    attn_gain_grad, mlp_gain_grad = gain_total[:share], gain_total[share : 2 * share]
    query_gain_grad = gain_total[2 * share : 2 * share + head_dim]
    key_gain_grad = gain_total[2 * share + head_dim :]
    return (
        layer_out,
        tokens_grad,
        query_wgrad,
        key_wgrad,
        value_wgrad,
        output_wgrad,
        attn_gain_grad,
        query_gain_grad,
        key_gain_grad,
        mlp_gain_grad,
        router_wgrad[:, :total_experts],
        jnp.swapaxes(place_experts(gate_blocks), 1, 2),
        jnp.swapaxes(place_experts(up_blocks), 1, 2),
        down_wgrad,
    )


def solution(mesh):
    in_specs = (
        P("ep", None),
        P("ep"),
        P("ep", None),
        P(None, "tp"),
        P(None, "tp"),
        P(None, "tp"),
        P(None, "tp"),
        P(),
        P(),
        P(),
        P(),
        P(),
        P("ep", None, "tp"),
        P("ep", None, "tp"),
        P("ep", "tp", None),
        P("ep", None),
    )
    out_specs = (
        P("ep", None),
        P("ep", None),
        P("ep", "tp"),
        P("ep", "tp"),
        P("ep", "tp"),
        P("ep", "tp"),
        P("ep"),
        P(),
        P(),
        P("ep"),
        P("ep", None),
        P("ep", None, "tp"),
        P("ep", None, "tp"),
        P("ep", "tp", None),
    )
    return jax.shard_map(
        per_device, mesh=mesh, in_specs=in_specs, out_specs=out_specs, check_vma=False
    )
```

```python
import math

import jax
import jax.numpy as jnp
from jax import lax
from jax.experimental import pallas as pl
from jax.experimental.pallas import tpu as pltpu
from jax.sharding import PartitionSpec as P

EPSILON = 1e-06
THETA = 1000000.0
MASKED = -1e30
PROJECT_FIRST, PROJECT_LAST = 100.0, 1.0
HALVES_FIRST, HALVES_LATER = 0.1, 100.0
BF = jnp.bfloat16
F32 = jnp.float32
COLS = (((1,), (1,)), ((), ()))
ROWS = (((0,), (0,)), ((), ()))


def norm_rate(value_rows):
    return lax.rsqrt(jnp.mean(value_rows * value_rows, axis=-1, keepdims=True) + EPSILON)


def norm_back(value_rows, rate, gain, upstream):
    scaled = upstream * gain
    inner = jnp.mean(scaled * value_rows, axis=-1, keepdims=True)
    return rate * scaled - value_rows * (rate * rate * rate) * inner


def rope_tables(doc_ids, head_dim):
    half_dim = head_dim // 2
    starts = jnp.sum((doc_ids[None, :] < doc_ids[:, None]).astype(jnp.int32), axis=1)
    places = jnp.arange(doc_ids.shape[0], dtype=jnp.int32) - starts
    inverse = THETA ** (-jnp.arange(half_dim, dtype=F32) * 2.0 / head_dim)
    angles = places.astype(F32)[:, None] * inverse[None, :]
    cosine, sine = jnp.cos(angles), jnp.sin(angles)
    return (
        jnp.concatenate([cosine, cosine], axis=1),
        jnp.concatenate([-sine, sine], axis=1),
    )


def fixed(shape):
    return pl.BlockSpec(shape, lambda i: (0,) * len(shape))


def cost(flops, bytes_accessed, weight=1.0):
    return pl.CostEstimate(
        flops=int(flops * weight) + 1, bytes_accessed=int(bytes_accessed * weight) + 1, transcendentals=0
    )


def joined(*groups):
    flat = lax.optimization_barrier(tuple(value for group in groups for value in group))
    result, at = [], 0
    for group in groups:
        result.append(list(flat[at : at + len(group)]))
        at += len(group)
    return result


def params():
    return pltpu.CompilerParams(vmem_limit_bytes=60 * 2**20)


def turn(rows, cos, sin):
    return rows * cos + pltpu.roll(rows, rows.shape[1] // 2, 1) * sin


def turn_back(rows, cos, sin):
    return rows * cos - pltpu.roll(rows, rows.shape[1] // 2, 1) * sin


def attend_kernel(
    head_dim, scale,
    tokens_ref, gain_ref, query_ref, key_ref, value_ref, column_ref, row_ref, cos_ref, sin_ref, query_gain_ref, key_gain_ref,
    normed_ref, rate_ref, heads_ref, query_raw_ref, query_low_ref, probs_ref, key_raw_ref, key_low_ref, value_low_ref,
    bias_ref, value_turned_ref,
):
    length = tokens_ref.shape[0]

    @pl.when(pl.program_id(0) == 0)
    def _():
        wide = tokens_ref[...].astype(F32)
        rate = norm_rate(wide)
        rate_ref[...] = jnp.broadcast_to(rate, rate_ref.shape)
        normed_ref[...] = (wide * rate * gain_ref[...]).astype(BF)
        keys = jnp.dot(normed_ref[...], key_ref[...], preferred_element_type=F32)
        key_raw_ref[...] = keys
        key_low_ref[...] = turn(
            keys * norm_rate(keys) * key_gain_ref[...], cos_ref[...], sin_ref[...]
        ).astype(BF)
        values = jnp.dot(normed_ref[...], value_ref[...], preferred_element_type=F32)
        value_low_ref[...] = values.astype(BF)
        value_turned_ref[...] = values.T.astype(BF)
        key_place = lax.broadcasted_iota(jnp.int32, (length, length), 0)
        query_place = lax.broadcasted_iota(jnp.int32, (length, length), 1)
        allowed = (key_place <= query_place) & (column_ref[...] == row_ref[...])
        bias_ref[...] = jnp.where(allowed, 0.0, MASKED)

    query_raw = jnp.dot(normed_ref[...], query_ref[...], preferred_element_type=F32)
    query_raw_ref[...] = query_raw
    for head in range(query_raw.shape[1] // head_dim):
        span = slice(head * head_dim, (head + 1) * head_dim)
        query = query_raw[:, span]
        query_low = turn(
            query * norm_rate(query) * query_gain_ref[...], cos_ref[...], sin_ref[...]
        ).astype(BF)
        query_low_ref[:, span] = query_low
        scores = (
            lax.dot_general(key_low_ref[...], query_low, COLS, preferred_element_type=F32) * scale
            + bias_ref[...]
        )
        exps = jnp.exp(scores - jnp.max(scores, axis=0, keepdims=True))
        probs = exps * (1.0 / jnp.sum(exps, axis=0, keepdims=True))
        probs_ref[head] = probs
        mixed = jnp.dot(value_turned_ref[...], probs.astype(BF), preferred_element_type=F32)
        heads_ref[:, span] = mixed.T.astype(BF)


def attend(
    tokens, doc_ids, query_weight, key_matrix, value_matrix, attn_gain, query_gain, key_gain, cos, sin, weight=1.0
):
    length, width = tokens.shape
    head_dim = query_gain.shape[0]
    cols = query_weight.shape[1]
    step = min(2 * head_dim, cols)
    heads = cols // head_dim
    narrow = pl.BlockSpec((length, step), lambda i: (0, i))
    single = fixed((length, head_dim))
    return pl.pallas_call(
        lambda *refs: attend_kernel(head_dim, 1.0 / math.sqrt(head_dim), *refs),
        grid=(cols // step,),
        in_specs=[
            fixed((length, width)), fixed((1, width)),
            pl.BlockSpec((width, step), lambda i: (0, i)),
            fixed((width, head_dim)), fixed((width, head_dim)),
            fixed((length, 1)), fixed((1, length)), single, single,
            fixed((1, head_dim)), fixed((1, head_dim)),
        ],
        out_specs=[
            fixed((length, width)), single, narrow, narrow, narrow,
            pl.BlockSpec((step // head_dim, length, length), lambda i: (i, 0, 0)),
            single, single, single,
        ],
        out_shape=[
            jax.ShapeDtypeStruct((length, width), BF),
            jax.ShapeDtypeStruct((length, head_dim), F32),
            jax.ShapeDtypeStruct((length, cols), BF),
            jax.ShapeDtypeStruct((length, cols), F32),
            jax.ShapeDtypeStruct((length, cols), BF),
            jax.ShapeDtypeStruct((heads, length, length), F32),
            jax.ShapeDtypeStruct((length, head_dim), F32),
            jax.ShapeDtypeStruct((length, head_dim), BF),
            jax.ShapeDtypeStruct((length, head_dim), BF),
        ],
        scratch_shapes=[pltpu.VMEM((length, length), F32), pltpu.VMEM((head_dim, length), BF)],
        compiler_params=params(),
        cost_estimate=cost(2 * length * width * cols, 2 * width * cols, weight),
    )(
        tokens, attn_gain[None, :], query_weight, key_matrix, value_matrix,
        doc_ids[:, None], doc_ids[None, :], cos, sin, query_gain[None, :], key_gain[None, :],
    )


def norm_parts(raw, gain, upstream):
    rate = norm_rate(raw)
    gain_grad = jnp.sum(upstream * raw * rate, axis=0, keepdims=True)
    return norm_back(raw, rate, gain, upstream), gain_grad


def gather_rows(blocks, *whole_refs):
    count, me = len(blocks), lax.axis_index("tp")
    size = blocks[0].shape[0]
    for shift, block in enumerate(blocks):
        start = pl.multiple_of((me + count - shift) % count * size, size)
        first = 0
        for whole_ref in whole_refs:
            last = first + whole_ref.shape[1]
            whole_ref[pl.ds(start, size), :] = block[:, first:last]
            first = last


def attend_back_kernel(
    count, head_dim, scale, *refs
):
    blocks = refs[:count]
    (
        out_ref, query_raw_ref, query_low_ref, probs_ref, key_raw_ref, key_low_ref, value_low_ref, cos_ref, sin_ref, query_gain_ref, key_gain_ref,
        branch_ref, logit_ref, grads_ref, gains_ref,
        key_turned_ref, key_sum, value_sum,
    ) = refs[count:]
    step = pl.program_id(0)
    cols = query_raw_ref.shape[1]

    @pl.when(step == 0)
    def _():
        gather_rows(blocks, branch_ref, logit_ref)
        key_turned_ref[...] = key_low_ref[...].astype(F32).T.astype(BF)
        key_sum[...] = jnp.zeros_like(key_sum)
        value_sum[...] = jnp.zeros_like(value_sum)
        gains_ref[...] = jnp.zeros_like(gains_ref)

    heads_grad = jnp.dot(branch_ref[...], out_ref[...], preferred_element_type=F32).astype(BF)
    cos, sin = cos_ref[...], sin_ref[...]
    for head in range(cols // head_dim):
        span = slice(head * head_dim, (head + 1) * head_dim)
        upstream = heads_grad[:, span]
        probs = probs_ref[head]
        prob_grad = lax.dot_general(
            value_low_ref[...], upstream, COLS, preferred_element_type=F32
        )
        delta = jnp.sum(probs * prob_grad, axis=0, keepdims=True)
        score_grad = (probs * (prob_grad - delta)).astype(BF)
        value_sum[...] += jnp.dot(probs.astype(BF), upstream, preferred_element_type=F32)
        key_sum[...] += jnp.dot(score_grad, query_low_ref[:, span], preferred_element_type=F32)
        turned = jnp.dot(key_turned_ref[...], score_grad, preferred_element_type=F32)
        query_back = (turned.T * scale).astype(BF).astype(F32)
        grad, gain = norm_parts(
            query_raw_ref[:, span], query_gain_ref[...], turn_back(query_back, cos, sin)
        )
        gains_ref[0:1, :] += gain
        start = pl.multiple_of(step * cols + head * head_dim, head_dim)
        grads_ref[:, pl.ds(start, head_dim)] = grad.astype(BF)

    @pl.when(step == pl.num_programs(0) - 1)
    def _():
        key_back = (key_sum[...] * scale).astype(BF).astype(F32)
        grad, gain = norm_parts(key_raw_ref[...], key_gain_ref[...], turn_back(key_back, cos, sin))
        gains_ref[1:2, :] += gain
        last = grads_ref.shape[1]
        grads_ref[:, last - 2 * head_dim : last - head_dim] = grad.astype(BF)
        grads_ref[:, last - head_dim :] = value_sum[...].astype(BF)


def attend_back(
    blocks, output_weight, query_raw, query_low, probs, key_raw, key_low, value_low, cos, sin, query_gain, key_gain, weight=0.1
):
    count, (size, wide), width = len(blocks), blocks[0].shape, output_weight.shape[0]
    length, cols = query_raw.shape
    head_dim = query_gain.shape[0]
    step = min(2 * head_dim, cols)
    single = fixed((length, head_dim))
    narrow = pl.BlockSpec((length, step), lambda i: (0, i))
    return pl.pallas_call(
        lambda *refs: attend_back_kernel(count, head_dim, 1.0 / math.sqrt(head_dim), *refs),
        grid=(cols // step,),
        in_specs=[fixed((size, wide))] * count
        + [
            pl.BlockSpec((width, step), lambda i: (0, i)), narrow, narrow,
            pl.BlockSpec((step // head_dim, length, length), lambda i: (i, 0, 0)),
            single, single, single, single, single, fixed((1, head_dim)), fixed((1, head_dim)),
        ],
        out_specs=[
            fixed((length, width)), fixed((length, wide - width)),
            fixed((length, cols + 2 * head_dim)), fixed((8, head_dim)),
        ],
        out_shape=[
            jax.ShapeDtypeStruct((length, width), BF),
            jax.ShapeDtypeStruct((length, wide - width), BF),
            jax.ShapeDtypeStruct((length, cols + 2 * head_dim), BF),
            jax.ShapeDtypeStruct((8, head_dim), F32),
        ],
        scratch_shapes=[
            pltpu.VMEM((head_dim, length), BF),
            pltpu.VMEM((length, head_dim), F32),
            pltpu.VMEM((length, head_dim), F32),
        ],
        compiler_params=params(),
        cost_estimate=cost(2 * length * width * cols, 2 * width * cols, weight),
    )(
        *blocks, output_weight, query_raw, query_low, probs, key_raw, key_low, value_low, cos, sin,
        query_gain[None, :], key_gain[None, :],
    )


def route_kernel(
    capacity, tp_count,
    routes_ref, turned_ref, rows_ref,
    mask_ref, turned_mask_ref, routed_ref, sent_ref,
    places_ref,
):
    length, top_count = routes_ref.shape
    experts, slots = routed_ref.shape[1], mask_ref.shape[1]
    owners = slots // capacity
    step, tile = pl.program_id(0), turned_mask_ref.shape[0]
    me = lax.axis_index("tp")

    def iota(shape, axis):
        return lax.broadcasted_iota(jnp.int32, shape, axis)

    def low(flags):
        return flags.astype(F32).astype(BF)

    @pl.when(step == 0)
    def _():
        expert = iota((length, experts), 1)
        routed = jnp.zeros((length, experts), F32)
        turned = jnp.zeros((experts, length), F32)
        for k in range(top_count):
            routed += (routes_ref[:, k : k + 1] == expert).astype(F32)
            turned += (turned_ref[k : k + 1, :] == iota((experts, length), 0)).astype(F32)
        routed_ref[...] = routed.astype(BF)
        own = jnp.dot(
            routed_ref[...],
            low(iota((experts, owners), 0) == iota((experts, owners), 1) * tp_count + me),
            preferred_element_type=F32,
        )
        earlier = low(iota((length, length), 0) > iota((length, length), 1))
        rank = jnp.dot(earlier, own.astype(BF), preferred_element_type=F32)
        places = jnp.where(own > 0.5, rank, -1.0).astype(BF)
        slot = iota((owners, slots), 1)
        wide = jnp.dot(
            places, low(lax.div(slot, capacity) == iota((owners, slots), 0)), preferred_element_type=F32
        )
        mask_ref[...] = low(wide == lax.rem(iota((1, slots), 1), capacity).astype(F32))
        own_turned = jnp.dot(
            low(iota((owners, experts), 1) == iota((owners, experts), 0) * tp_count + me),
            turned.astype(BF),
            preferred_element_type=F32,
        )
        later = low(iota((length, length), 0) < iota((length, length), 1))
        rank_turned = jnp.dot(own_turned.astype(BF), later, preferred_element_type=F32)
        places_ref[...] = jnp.where(own_turned > 0.5, rank_turned, -1.0).astype(BF)

    slot = iota((tile, owners), 0) + step * tile
    wide = jnp.dot(
        low(lax.div(slot, capacity) == iota((tile, owners), 1)), places_ref[...], preferred_element_type=F32
    )
    mask = low(wide == lax.rem(iota((tile, 1), 0) + step * tile, capacity).astype(F32))
    turned_mask_ref[...] = mask
    width = rows_ref.shape[1]
    sent_ref[:, :width] = jnp.dot(mask, rows_ref[...], preferred_element_type=F32).astype(BF)
    sent_ref[:, width:] = jnp.dot(mask, routed_ref[...], preferred_element_type=F32).astype(BF)


def route(routes, rows, experts, capacity, ep_count, tp_count, weight=1.0):
    (length, top_count), width = routes.shape, rows.shape[1]
    slots = ep_count * capacity
    tile = min(256, slots)
    return pl.pallas_call(
        lambda *refs: route_kernel(capacity, tp_count, *refs),
        grid=(slots // tile,),
        in_specs=[fixed((length, top_count)), fixed((top_count, length)), fixed((length, width))],
        out_specs=[
            fixed((length, slots)),
            pl.BlockSpec((tile, length), lambda i: (i, 0)),
            fixed((length, experts)),
            pl.BlockSpec((tile, width + experts), lambda i: (i, 0)),
        ],
        out_shape=[
            jax.ShapeDtypeStruct((length, slots), BF),
            jax.ShapeDtypeStruct((slots, length), BF),
            jax.ShapeDtypeStruct((length, experts), BF),
            pltpu.HBM((slots, width + experts), BF),
        ],
        scratch_shapes=[pltpu.VMEM((ep_count, length), BF)],
        compiler_params=params(),
        cost_estimate=cost(2 * length * slots * width, 2 * slots * width, weight),
    )(routes, routes.T, rows)


def gate_kernel(capacity, tp_count, rows_ref, router_ref, routed_ref, mask_ref, probs_ref, weight_ref):
    experts, slots = routed_ref.shape[1], mask_ref.shape[1]
    owners = slots // capacity
    me = lax.axis_index("tp")

    def iota(shape, axis):
        return lax.broadcasted_iota(jnp.int32, shape, axis)

    logits = jnp.dot(rows_ref[...], router_ref[...], preferred_element_type=F32)
    logits = jnp.where(routed_ref[...].astype(F32) > 0.5, logits, MASKED)
    exps = jnp.exp(logits - jnp.max(logits, axis=1, keepdims=True))
    probs = exps / jnp.sum(exps, axis=1, keepdims=True)
    probs_ref[...] = probs
    spread = (
        iota((experts, slots), 0) == lax.div(iota((experts, slots), 1), capacity) * tp_count + me
    )
    weights = jnp.dot(
        probs.astype(BF), spread.astype(F32).astype(BF), preferred_element_type=F32
    )
    weight_ref[...] = weights.astype(BF) * mask_ref[...]


def gate_weights(rows, router_weight, routed, mask, capacity, ep_count, tp_count, weight=1.0):
    length, slots = mask.shape
    return pl.pallas_call(
        lambda *refs: gate_kernel(capacity, tp_count, *refs),
        out_shape=[
            jax.ShapeDtypeStruct(routed.shape, F32),
            jax.ShapeDtypeStruct((length, slots), BF),
        ],
        compiler_params=params(),
        cost_estimate=cost(2 * length * routed.shape[1] * (rows.shape[1] + slots), 4 * length * slots, weight),
    )(rows, router_weight, routed, mask)


def fill_kernel(count, *refs):
    blocks, (mask_ref, sent_ref, whole_ref) = refs[:count], refs[count:]

    @pl.when(pl.program_id(0) == 0)
    def _():
        gather_rows(blocks, whole_ref)

    sent_ref[...] = jnp.dot(mask_ref[...], whole_ref[...], preferred_element_type=F32).astype(BF)


def fill(blocks, turned_mask, weight=0.1):
    count, (size, width) = len(blocks), blocks[0].shape
    slots, length = turned_mask.shape
    tile = min(256, slots)
    return pl.pallas_call(
        lambda *refs: fill_kernel(count, *refs),
        grid=(slots // tile,),
        in_specs=[fixed((size, width))] * count + [pl.BlockSpec((tile, length), lambda i: (i, 0))],
        out_specs=[pl.BlockSpec((tile, width), lambda i: (i, 0)), fixed((length, width))],
        out_shape=[
            pltpu.HBM((slots, width), BF),
            jax.ShapeDtypeStruct((length, width), BF),
        ],
        compiler_params=params(),
        cost_estimate=cost(2 * length * slots * width, 2 * slots * width, weight),
    )(*blocks, turned_mask)


def after(value, *earlier):
    return lax.optimization_barrier((value,) + earlier)[0]


def ring(count, shift):
    return [(i, (i + shift) % count) for i in range(count)]


def row_block(value_rows, index, count):
    size = value_rows.shape[0] // count
    return lax.dynamic_slice_in_dim(value_rows, index * size, size, 0)


def tp_spread(block):
    count = lax.axis_size("tp")
    return [block] + [lax.ppermute(block, "tp", ring(count, shift)) for shift in range(1, count)]


def tp_join(blocks):
    count, me = lax.axis_size("tp"), lax.axis_index("tp")
    whole = jnp.zeros((count,) + blocks[0].shape, blocks[0].dtype)
    for shift, block in enumerate(blocks):
        whole = lax.dynamic_update_index_in_dim(whole, block, (me - shift) % count, 0)
    return whole.reshape((-1,) + blocks[0].shape[1:])


def tp_sum_blocks(blocks):
    count = lax.axis_size("tp")
    total = blocks[0].astype(F32)
    for shift in range(1, count):
        total = total + lax.ppermute(blocks[shift], "tp", ring(count, shift)).astype(F32)
    return total


def project_kernel(count, spans, left_ref, *refs):
    rights, refs = refs[: len(spans)], refs[len(spans) :]
    outs, held = refs[-count - 1 : -1], refs[-1]
    me = lax.axis_index("tp")
    size = left_ref.shape[0] // count
    for right_ref, (first, last) in zip(rights, spans):
        got = lax.dot_general(
            left_ref[:, first:last], right_ref[...], COLS, preferred_element_type=F32
        )
        if first == 0:
            held[...] = got
        else:
            held[...] += got
    for shift in range(count):
        start = pl.multiple_of((me + shift) % count * size, size)
        outs[shift][...] = held[pl.ds(start, size), :].astype(BF)
    if len(refs) > count + 1:
        rows_ref, rate_ref, gain_ref = refs[:3]
        gain_ref[...] = jnp.sum(
            held[...] * (rows_ref[...].astype(F32) * rate_ref[:, :1]), axis=0, keepdims=True
        )


def project(left, rights, rows=None, rate=None, tile=512, weight=1.0):
    count = lax.axis_size("tp")
    length, width = left.shape[0], rights[0].shape[0]
    tile = min(tile, width)
    spans, first = [], 0
    for right in rights:
        spans.append((first, first + right.shape[1]))
        first += right.shape[1]
    size = length // count
    in_specs = [fixed(left.shape)]
    in_specs += [pl.BlockSpec((tile, right.shape[1]), lambda i: (i, 0)) for right in rights]
    out_specs = [pl.BlockSpec((size, tile), lambda i: (0, i))] * count
    out_shape = [jax.ShapeDtypeStruct((size, width), BF)] * count
    more = []
    if rows is not None:
        more = [rows, rate]
        in_specs += [pl.BlockSpec((length, tile), lambda i: (0, i)), fixed(rate.shape)]
        out_specs = [pl.BlockSpec((1, tile), lambda i: (0, i))] + out_specs
        out_shape = [jax.ShapeDtypeStruct((1, width), F32)] + out_shape
    return pl.pallas_call(
        lambda *refs: project_kernel(count, spans, *refs),
        grid=(width // tile,),
        in_specs=in_specs,
        out_specs=out_specs,
        out_shape=out_shape,
        scratch_shapes=[pltpu.VMEM((length, tile), F32)],
        compiler_params=params(),
        cost_estimate=cost(2 * length * first * width, 2 * first * width, weight),
    )(left, *rights, *more)


def expert_kernel(
    width, rows_ref, grads_ref, *refs
):
    count = (len(refs) - 7) // 2
    sources = [refs[:count], refs[count : 2 * count]]
    back_ref, act_ref, gate_back_ref, up_back_ref, *held, sems = refs[2 * count :]
    size = sources[0][0].shape[0]

    def loads(which):
        return [
            pltpu.make_async_copy(
                source, held[which].at[pl.ds(part * size, size), :], sems.at[which, part]
            )
            for part, source in enumerate(sources[which])
        ]

    first = pl.program_id(0) == 0

    @pl.when(first)
    def _():
        for which in range(2):
            for load in loads(which):
                load.start()
        for load in loads(0):
            load.wait()

    rows = rows_ref[...]
    gate_val = lax.dot_general(rows, held[0][...], COLS, preferred_element_type=F32)

    @pl.when(first)
    def _():
        for load in loads(1):
            load.wait()

    up_val = lax.dot_general(rows, held[1][...], COLS, preferred_element_type=F32)

    act_grad = grads_ref[...]
    gate_sig = jax.nn.sigmoid(gate_val)
    gate_act = gate_val * gate_sig
    act_low = (gate_act * up_val).astype(BF)
    act_ref[...] = act_low
    gate_back = (act_grad * up_val * gate_sig * (1.0 + gate_val * (1.0 - gate_sig))).astype(BF)
    up_back = (act_grad * gate_act).astype(BF)
    gate_back_ref[...] = gate_back
    up_back_ref[...] = up_back
    slot_grad = jnp.sum(act_low.astype(F32) * act_grad, axis=1, keepdims=True)
    back_ref[:, width:] = jnp.broadcast_to(
        slot_grad, (rows.shape[0], back_ref.shape[1] - width)
    ).astype(BF)
    back_ref[:, :width] = (
        jnp.dot(gate_back, held[0][...], preferred_element_type=F32)
        + jnp.dot(up_back, held[1][...], preferred_element_type=F32)
    ).astype(BF)


def hidden_kernel(rows_ref, *refs):
    blocks, out_ref = refs[:-1], refs[-1]
    size = blocks[0].shape[0]
    for part, block in enumerate(blocks):
        out_ref[:, part * size : (part + 1) * size] = lax.dot_general(
            rows_ref[...], block[...], COLS, preferred_element_type=F32
        )


def hidden_grads(rows, downs, tile=256, weight=10.0):
    slots, (size, width) = rows.shape[0], downs[0].shape
    tile = min(tile, slots)
    return pl.pallas_call(
        hidden_kernel,
        grid=(slots // tile,),
        in_specs=[pl.BlockSpec((tile, width), lambda i: (i, 0))] + [fixed((size, width))] * len(downs),
        out_specs=pl.BlockSpec((tile, size * len(downs)), lambda i: (i, 0)),
        out_shape=pltpu.HBM((slots, size * len(downs)), F32),
        compiler_params=params(),
        cost_estimate=cost(2 * slots * width * size * len(downs), 2 * slots * width, weight),
    )(rows, *downs)


def expert_pass(rows_in, act_grad, gates, ups, extra, tile=256, weight=1.0):
    slots, width = rows_in.shape
    tile = min(tile, slots)
    hidden = len(gates) * gates[0].shape[0]
    tall = pl.BlockSpec((tile, width), lambda i: (i, 0))
    narrow = pl.BlockSpec((tile, hidden), lambda i: (i, 0))
    low = jax.ShapeDtypeStruct((slots, hidden), BF)
    return pl.pallas_call(
        lambda *refs: expert_kernel(width, *refs),
        grid=(slots // tile,),
        in_specs=[tall, narrow] + [pl.BlockSpec(memory_space=pl.ANY)] * (2 * len(gates)),
        out_specs=[pl.BlockSpec((tile, width + extra), lambda i: (i, 0)), narrow, narrow, narrow],
        out_shape=[pltpu.HBM((slots, width + extra), BF), low, low, low],
        scratch_shapes=[pltpu.VMEM((hidden, width), BF)] * 2
        + [pltpu.SemaphoreType.DMA((2, len(gates)))],
        compiler_params=params(),
        cost_estimate=cost(8 * slots * width * hidden, 6 * slots * width + 6 * width * hidden, weight),
    )(rows_in, act_grad, *gates, *ups)


def place_kernel(count, *refs):
    ins, out_ref = refs[:count], refs[count]
    step = pl.program_id(0)
    for shift in range(count):

        @pl.when(step == shift)
        def _():
            out_ref[0] = ins[shift][...].astype(out_ref.dtype)


def place_blocks(blocks, direction, dtype, tile, weight=1.0):
    count, me = len(blocks), lax.axis_index("tp")
    rows, cols = blocks[0].shape
    steps = rows // tile

    def held(shift):
        return lambda s, t, me_ref: (jnp.where(s < shift, 0, jnp.where(s > shift, steps - 1, t)), 0)

    return pl.pallas_call(
        lambda me_ref, *refs: place_kernel(count, *refs),
        grid_spec=pltpu.PrefetchScalarGridSpec(
            num_scalar_prefetch=1,
            grid=(count, steps),
            in_specs=[pl.BlockSpec((tile, cols), held(shift)) for shift in range(count)],
            out_specs=pl.BlockSpec(
                (1, tile, cols), lambda s, t, me_ref: ((me_ref[0] + direction * s + count) % count, t, 0)
            ),
        ),
        out_shape=jax.ShapeDtypeStruct((count, rows, cols), dtype),
        compiler_params=params(),
        cost_estimate=cost(0, count * rows * cols * (2 + jnp.dtype(dtype).itemsize), weight),
    )(me.astype(jnp.int32).reshape(1), *blocks)


def pull_slices(weights, picks):
    count, me = lax.axis_size("tp"), lax.axis_index("tp")
    return [
        lax.dynamic_index_in_dim(weights[which], (me + shift) % count, 0, keepdims=False)
        for which, shift in picks
    ]


def shift_blocks(blocks, shifts):
    count = lax.axis_size("tp")
    return [
        lax.ppermute(block, "tp", ring(count, shift)) for block, shift in zip(blocks, shifts)
    ]


def push_blocks(grad, shifts=None):
    count = lax.axis_size("tp")
    size = grad.shape[0] // count
    blocks = []
    for shift in range(count) if shifts is None else shifts:
        block = grad[shift * size : (shift + 1) * size]
        blocks.append(lax.ppermute(block, "tp", ring(count, -shift)) if shift else block)
    return blocks


def place_experts(blocks):
    return place_blocks(blocks, 1, F32, blocks[0].shape[0])


def ep_exchange(rows):
    return lax.all_to_all(rows, "ep", 0, 0, tiled=True)


def wgrad_kernel(share, spans, *refs):
    count = len(spans)
    lefts, rights, (keep_ref, send_ref, held) = refs[:count], refs[count : 2 * count], refs[2 * count :]
    core = lax.axis_index("ep") % 2
    for left_ref, right_ref, (first, size) in zip(lefts, rights, spans):
        held[:, first : first + size] = lax.dot_general(
            left_ref[...], right_ref[...], ROWS, preferred_element_type=F32
        )
    split_cores(share, core, held, keep_ref, send_ref)


def split_cores(share, core, held, keep_ref, send_ref):
    for chip in range(held.shape[0] // (2 * share)):
        kept = pl.multiple_of((2 * chip + core) * share, share)
        sent = pl.multiple_of((2 * chip + 1 - core) * share, share)
        keep_ref[chip * share : (chip + 1) * share, :] = held[pl.ds(kept, share), :].astype(BF)
        send_ref[chip * share : (chip + 1) * share, :] = held[pl.ds(sent, share), :].astype(BF)


def grad_halves(pairs, tile=512, weight=1.0):
    count = lax.axis_size("ep")
    length, width = pairs[0][0].shape
    share = width // count
    tile = min(tile, width)
    spans, cols = [], 0
    for _, right in pairs:
        spans.append((cols, right.shape[1]))
        cols += right.shape[1]
    half = pl.BlockSpec((tile // 2, cols), lambda i: (i, 0))
    return pl.pallas_call(
        lambda *refs: wgrad_kernel(share, spans, *refs),
        grid=(width // tile,),
        in_specs=[pl.BlockSpec((length, tile), lambda i: (0, i))] * len(pairs)
        + [pl.BlockSpec(right.shape, lambda i: (0, 0)) for _, right in pairs],
        out_specs=[half, half],
        out_shape=[pltpu.HBM((width // 2, cols), BF)] * 2,
        scratch_shapes=[pltpu.VMEM((tile, cols), F32)],
        compiler_params=params(),
        cost_estimate=cost(2 * length * width * cols, 3 * width * cols, weight),
    )(*[left for left, _ in pairs], *[right for _, right in pairs])


def swap_cores(value):
    return lax.ppermute(value, "ep", [(i, i ^ 1) for i in range(lax.axis_size("ep"))])


def pair_kernel(share, first_keep, first_got, second_keep, second_got, extra_ref, out_ref):
    for chip in range(out_ref.shape[0]):
        rows, row = slice(chip * share, (chip + 1) * share), 0
        for keep_ref, got_ref in ((first_keep, first_got), (second_keep, second_got)):
            for column in range(0, keep_ref.shape[1], 128):
                span = slice(column, column + 128)
                both = keep_ref[rows, span].astype(F32) + got_ref[rows, span].astype(F32)
                out_ref[chip, row : row + share, :] = both.astype(BF)
                row += share
        out_ref[chip, row:, :] = extra_ref[chip]


def pair_sums(pairs, extra, weight=1.0):
    chips = extra.shape[0]
    share = pairs[0][0].shape[0] // chips
    step = min(4, chips)
    blocks = [pl.BlockSpec((step * share, keep.shape[1]), lambda i: (i, 0)) for keep, _ in pairs for _ in range(2)]
    rows = sum(keep.shape[1] // 128 * share for keep, _ in pairs) + extra.shape[1]
    return pl.pallas_call(
        lambda *refs: pair_kernel(share, *refs),
        grid=(chips // step,),
        in_specs=blocks + [pl.BlockSpec((step,) + extra.shape[1:], lambda i: (i, 0, 0))],
        out_specs=pl.BlockSpec((step, rows, 128), lambda i: (i, 0, 0)),
        out_shape=pltpu.HBM((chips, rows, 128), BF),
        compiler_params=params(),
        cost_estimate=cost(0, 8 * chips * rows * 128, weight),
    )(*[value for pair in pairs for value in pair], extra)


def chip_kernel(widths, parts_ref, *outs):
    share, row = outs[0].shape[0], 0
    for out_ref, width in zip(outs, widths):
        for column in range(0, width, 128):
            part = parts_ref[:, row : row + share, :].astype(F32)
            out_ref[:, column : column + 128] = jnp.sum(part, axis=0)
            row += share
    outs[-1][...] = jnp.sum(parts_ref[:, row:, :].astype(F32), axis=0)


def chip_sums(parts, widths, share, weight=1.0):
    rest = parts.shape[1] - sum(widths) // 128 * share
    return pl.pallas_call(
        lambda *refs: chip_kernel(widths, *refs),
        out_shape=[jax.ShapeDtypeStruct((share, width), F32) for width in widths]
        + [jax.ShapeDtypeStruct((rest, 128), F32)],
        compiler_params=params(),
        cost_estimate=cost(0, 2 * parts.size, weight),
    )(parts)


def chip_exchange(parts):
    count = lax.axis_size("ep")
    if count == 2:
        return parts
    groups = [list(range(side, count, 2)) for side in range(2)]
    return lax.all_to_all(parts, "ep", 0, 0, axis_index_groups=groups, tiled=True)


def core_sum(extra):
    core, many = lax.axis_index("ep") % 2, extra.shape[1]
    extra = extra.reshape(-1, 2, many)
    total = lax.dynamic_index_in_dim(extra, core, 1, keepdims=False)
    total += swap_cores(lax.dynamic_index_in_dim(extra, 1 - core, 1, keepdims=False))
    total = total.reshape(total.shape[0], -1, 128)
    high = total.astype(BF)
    low = (total - high.astype(F32)).astype(BF)
    rows = jnp.concatenate([high, low], axis=1)
    return jnp.pad(rows, ((0, 0), (0, -rows.shape[1] % 8), (0, 0)))


def combine_kernel(count, capacity, width, weight_ref, mask_ref, rows_ref, *refs):
    outs, held = refs[:-1], refs[-1]
    me = lax.axis_index("tp")
    size = weight_ref.shape[0] // count
    shape = (rows_ref.shape[0], rows_ref.shape[1] - width)
    owner = lax.div(lax.broadcasted_iota(jnp.int32, shape, 0), capacity)
    named = owner * count + me == lax.broadcasted_iota(jnp.int32, shape, 1)
    held[:, :width] = jnp.dot(weight_ref[...], rows_ref[:, :width], preferred_element_type=F32)
    held[:, width:] = jnp.dot(
        mask_ref[...], rows_ref[:, width:] * named.astype(F32).astype(BF), preferred_element_type=F32
    )
    for shift in range(count):
        start = pl.multiple_of((me + shift) % count * size, size)
        outs[shift][...] = held[pl.ds(start, size), :].astype(BF)


def combine(weights, mask, rows, width, capacity, weight=0.0):
    count = lax.axis_size("tp")
    length, wide = weights.shape[0], rows.shape[1]
    return pl.pallas_call(
        lambda *refs: combine_kernel(count, capacity, width, *refs),
        out_shape=[jax.ShapeDtypeStruct((length // count, wide), BF)] * count,
        scratch_shapes=[pltpu.VMEM((length, wide), F32)],
        compiler_params=params(),
        cost_estimate=cost(2 * length * rows.shape[0] * wide, 2 * rows.shape[0] * wide, weight),
    )(weights, mask, rows)


def mix_kernel(count, weight_ref, rows_ref, *refs):
    outs, held = refs[:-1], refs[-1]
    me = lax.axis_index("tp")
    size = weight_ref.shape[0] // count
    held[...] = jnp.dot(weight_ref[...], rows_ref[...], preferred_element_type=F32)
    for shift in range(count):
        start = pl.multiple_of((me + shift) % count * size, size)
        outs[shift][...] = held[pl.ds(start, size), :].astype(BF)


def mix(weights, rows, tile=512, weight=10.0):
    count = lax.axis_size("tp")
    (length, slots), width = weights.shape, rows.shape[1]
    tile = min(tile, width)
    return pl.pallas_call(
        lambda *refs: mix_kernel(count, *refs),
        grid=(width // tile,),
        in_specs=[fixed((length, slots)), pl.BlockSpec((slots, tile), lambda i: (0, i))],
        out_specs=[pl.BlockSpec((length // count, tile), lambda i: (0, i))] * count,
        out_shape=[jax.ShapeDtypeStruct((length // count, width), BF)] * count,
        scratch_shapes=[pltpu.VMEM((length, tile), F32)],
        compiler_params=params(),
        cost_estimate=cost(2 * length * slots * width, 2 * slots * width, weight),
    )(weights, rows)


def tp_sum(value):
    count, total = lax.axis_size("tp"), value
    for shift in range(1, count):
        total = total + lax.ppermute(value, "tp", ring(count, shift))
    return total


def per_device(
    tokens,
    doc_ids,
    routes,
    query_weight,
    key_matrix,
    value_matrix,
    output_weight,
    attn_gain,
    query_gain,
    key_gain,
    mlp_gain,
    router_weight,
    gate_weight,
    up_weight,
    down_weight,
    cotangent,
):
    length, width = tokens.shape
    head_dim = query_gain.shape[0]
    total_experts = router_weight.shape[1]
    top_count = routes.shape[1]
    ep_count, tp_count = lax.axis_size("ep"), lax.axis_size("tp")
    ep_index, tp_index = lax.axis_index("ep"), lax.axis_index("tp")
    capacity = length * top_count * 4 // (3 * total_experts)
    slots = ep_count * capacity

    near, far = (1, tp_count - 1), range(2, tp_count - 1)
    weights = (jnp.swapaxes(gate_weight, 1, 2), jnp.swapaxes(up_weight, 1, 2), down_weight)
    near_gates_out = pull_slices(weights, [(0, shift) for shift in near])
    far_gates_out = pull_slices(weights, [(0, shift) for shift in far])
    near_ups_out = pull_slices(weights, [(1, shift) for shift in near])
    far_ups_out = pull_slices(weights, [(1, shift) for shift in far])
    near_downs_out = pull_slices(weights, [(2, shift) for shift in near])
    far_downs_out = pull_slices(weights, [(2, shift) for shift in far])
    (tokens,), near_gates_out, far_gates_out = joined((tokens,), near_gates_out, far_gates_out)
    (tokens,), near_gates_out = joined((tokens,), near_gates_out)
    near_gates = shift_blocks(near_gates_out, near)

    def dispatch(sent):
        return ep_exchange(sent.reshape(ep_count, capacity, -1)).reshape(slots, -1)

    (tokens,), = joined((tokens,))
    (tokens,), = joined((tokens,))
    cos, sin = rope_tables(doc_ids, head_dim)
    (
        first_normed, rate_first, heads_low, query_raw, query_low, probs, key_raw, key_low, value_low,
    ) = attend(
        tokens, doc_ids, query_weight, key_matrix, value_matrix, attn_gain, query_gain, key_gain, cos, sin
    )

    (cotangent, heads_low), = joined((cotangent, heads_low))
    (cotangent,), near_gates = joined((cotangent,), near_gates)
    (cotangent,), far_gates_out = joined((cotangent,), far_gates_out)
    far_gates = shift_blocks(far_gates_out, far)
    send_mask, turned_mask, routed, sent_grads = route(
        routes, cotangent, total_experts, capacity, ep_count, tp_count
    )
    (heads_low, sent_grads), = joined((heads_low, sent_grads))
    (sent_grads,), = joined((sent_grads,))
    (sent_grads,), = joined((sent_grads,))
    (heads_low,), far_gates = joined((heads_low,), far_gates)
    (heads_low,), = joined((heads_low,))
    attn_parts = project(heads_low, [output_weight], weight=PROJECT_FIRST)
    grads_in = dispatch(sent_grads)

    tokens_own = row_block(tokens, tp_index, tp_count).astype(F32)
    upstream_own = row_block(cotangent, tp_index, tp_count).astype(F32)
    hidden = tokens_own + tp_sum_blocks(attn_parts)
    rate_second = norm_rate(hidden)
    normed_own = (hidden * rate_second * mlp_gain).astype(BF)
    own = pull_slices(weights, [(0, 0), (1, 0), (2, 0)])
    (normed_own,), near_ups_out, far_ups_out, near_downs_out, far_downs_out = joined((normed_own,), near_ups_out, far_ups_out, near_downs_out, far_downs_out)
    (normed_own,), = joined((normed_own,))
    (normed_own,), near_ups_out, far_ups_out, near_downs_out = joined((normed_own,), near_ups_out, far_ups_out, near_downs_out)
    near_ups = shift_blocks(near_ups_out, near)
    far_ups = shift_blocks(far_ups_out, far)
    near_downs = shift_blocks(near_downs_out, near)
    normed_blocks = tp_spread(normed_own)
    normed_blocks, far_downs_out = joined(normed_blocks, far_downs_out)
    far_downs = shift_blocks(far_downs_out, far)
    normed_blocks, = joined(normed_blocks)
    sent_rows, normed_second = fill(normed_blocks, turned_mask)
    rows_in = dispatch(sent_rows)
    (normed_second,), far_downs = joined((normed_second,), far_downs)

    columns = jnp.arange(total_experts, dtype=jnp.int32)
    slot_logits = jnp.dot(rows_in, router_weight, preferred_element_type=F32)
    slot_logits = jnp.where(grads_in[:, width:].astype(F32) > 0.5, slot_logits, MASKED)
    slot_exp = jnp.exp(slot_logits - jnp.max(slot_logits, axis=-1, keepdims=True))
    own_expert = (columns == ep_index * tp_count + tp_index).astype(F32)
    probs_in = jnp.sum(slot_exp * own_expert[None, :], axis=-1) / jnp.sum(slot_exp, axis=-1)

    (grads_in,), near_downs = joined((grads_in,), near_downs)
    downs = [own[2], near_downs[0], *far_downs, near_downs[1]]
    down_full = jnp.concatenate(downs, axis=0)
    act_grad = hidden_grads(grads_in, downs)
    (act_grad,), near_ups, far_ups = joined((act_grad,), near_ups, far_ups)
    gates = [own[0], near_gates[0], *far_gates, near_gates[1]]
    ups = [own[1], near_ups[0], *far_ups, near_ups[1]]
    rows_grad, act_low, gate_back, up_back = expert_pass(rows_in, act_grad, gates, ups, total_experts)
    (normed_second, act_low), = joined((normed_second, act_low))
    gate_probs, weigh_back = gate_weights(
        normed_second, router_weight, routed, send_mask, capacity, ep_count, tp_count
    )
    back_rows = dispatch(rows_grad)
    expert_out = jnp.dot(act_low, down_full, preferred_element_type=F32).astype(BF)

    def expert_grad(left, right):
        weighed = (left.astype(F32) * probs_in[:, None]).astype(BF)
        return lax.dot_general(weighed, right, ROWS, preferred_element_type=F32).astype(BF)

    down_blocks = push_blocks(expert_grad(act_low, grads_in[:, :width]))
    gate_part = expert_grad(gate_back, rows_in)
    up_part = expert_grad(up_back, rows_in)
    unit = gate_part.shape[0] // tp_count

    def part_of(part, shift):
        return part[shift * unit : (shift + 1) * unit]

    own_parts = [part_of(gate_part, 0), part_of(up_part, 0)]
    gate_near = [part_of(gate_part, shift) for shift in near]
    up_near = [part_of(up_part, shift) for shift in near]
    far_parts = [
        jnp.concatenate([part_of(gate_part, shift), part_of(up_part, shift)], axis=0) for shift in far
    ]
    back_near, back_far = [-shift for shift in near], [-shift for shift in far]
    down_group = list(down_blocks)
    pushed_gates = shift_blocks(gate_near, back_near)
    held = (back_rows, expert_out, *down_group)
    held, pushed_gates, own_parts, up_near, far_parts = joined(held, pushed_gates, own_parts, up_near, far_parts)
    back_rows, expert_out, *down_group = held

    input_parts = combine(weigh_back, send_mask, back_rows, width, capacity)
    down_group, input_parts = joined(down_group, input_parts)
    down_wgrad = place_experts(down_group)
    expert_out, *input_parts = joined((expert_out, *input_parts))[0]
    returned = [dispatch(expert_out)]
    back_sum = tp_sum_blocks(input_parts)

    gate_grad = back_sum[:, width:]
    probs_own = row_block(gate_probs, tp_index, tp_count)
    gate_mean = jnp.sum(probs_own * gate_grad, axis=-1, keepdims=True)
    logit_own = (probs_own * (gate_grad - gate_mean)).astype(BF)
    router_input = lax.dot_general(logit_own, router_weight, COLS, preferred_element_type=F32)
    second_grad = router_input + back_sum[:, :width]
    mlp_gain_part = jnp.sum(second_grad * hidden * rate_second, axis=0)
    hidden_grad = upstream_own + norm_back(hidden, rate_second, mlp_gain, second_grad)
    branch_blocks = tp_spread(jnp.concatenate([hidden_grad.astype(BF), logit_own], axis=1))
    branch_blocks, up_near = joined(branch_blocks, up_near)
    pushed_ups = shift_blocks(up_near, back_near)
    branch_blocks, = joined(branch_blocks)

    branch_low, logit_grad, raw_grads, head_gains = attend_back(
        branch_blocks, output_weight, query_raw, query_low, probs, key_raw, key_low, value_low, cos, sin, query_gain, key_gain
    )
    (branch_low, raw_grads), = joined((branch_low, raw_grads))
    (raw_grads,), pushed_ups = joined((raw_grads,), pushed_ups)
    attn_gain_part, *first_parts = project(
        raw_grads, [query_weight, key_matrix, value_matrix], tokens, rate_first, weight=PROJECT_LAST
    )
    share = width // ep_count
    gains = jnp.concatenate(
        [
            attn_gain_part.reshape(ep_count, share),
            mlp_gain_part.reshape(ep_count, share),
            jnp.broadcast_to(head_gains[:2].reshape(1, -1), (ep_count, 2 * head_dim)),
        ],
        axis=1,
    )
    raw_keep, raw_send = grad_halves([(first_normed, raw_grads)], weight=HALVES_FIRST)
    raw_got = swap_cores(raw_send)
    extra = core_sum(gains)
    first_grad = tp_sum_blocks(first_parts)
    (first_grad,), returned = joined((first_grad,), returned)
    (first_grad, branch_low), = joined((first_grad, branch_low))
    (branch_low,), = joined((branch_low,))
    logits_wide = jnp.pad(logit_grad, ((0, 0), (0, -total_experts % 128)))
    later_pair = grad_halves([(branch_low, heads_low), (normed_second, logits_wide)], weight=HALVES_LATER)
    later_pair = (later_pair[0], swap_cores(later_pair[1]))
    (first_grad,), far_parts = joined((first_grad,), far_parts)
    pushed_far = shift_blocks(far_parts, back_far)
    sums = pair_sums([(raw_keep, raw_got), later_pair], extra)
    rate_own = row_block(rate_first, tp_index, tp_count)[:, :1]
    (first_grad, sums), = joined((first_grad, sums))
    tokens_own_grad = hidden_grad + norm_back(tokens_own, rate_own, attn_gain, first_grad)
    token_blocks = tp_spread(tokens_own_grad.astype(BF))
    token_blocks, = joined(token_blocks)
    tokens_grad = tp_join(token_blocks)

    returned, = joined(returned)
    layer_own = (hidden + tp_sum_blocks(mix(weigh_back, returned[0]))).astype(BF)
    (layer_own,), = joined((layer_own,))

    widths = (
        query_weight.shape[1], key_matrix.shape[1], value_matrix.shape[1], heads_low.shape[1], total_experts + -total_experts % 128,
    )
    query_wgrad, key_wgrad, value_wgrad, output_wgrad, router_wgrad, gain_rows = chip_sums(
        chip_exchange(sums), widths, share
    )
    many = gains.shape[1] // 128
    gain_total = tp_sum((gain_rows[:many] + gain_rows[many : 2 * many]).reshape(-1))
    layer_blocks = tp_spread(layer_own)
    gate_blocks = [own_parts[0], pushed_gates[0], *[block[:unit] for block in pushed_far], pushed_gates[1]]
    up_blocks = [own_parts[1], pushed_ups[0], *[block[unit:] for block in pushed_far], pushed_ups[1]]
    layer_out = tp_join(layer_blocks)
    attn_gain_grad, mlp_gain_grad = gain_total[:share], gain_total[share : 2 * share]
    query_gain_grad = gain_total[2 * share : 2 * share + head_dim]
    key_gain_grad = gain_total[2 * share + head_dim :]
    return (
        layer_out,
        tokens_grad,
        query_wgrad,
        key_wgrad,
        value_wgrad,
        output_wgrad,
        attn_gain_grad,
        query_gain_grad,
        key_gain_grad,
        mlp_gain_grad,
        router_wgrad[:, :total_experts],
        jnp.swapaxes(place_experts(gate_blocks), 1, 2),
        jnp.swapaxes(place_experts(up_blocks), 1, 2),
        down_wgrad,
    )


def solution(mesh):
    in_specs = (
        P("ep", None),
        P("ep"),
        P("ep", None),
        P(None, "tp"),
        P(None, "tp"),
        P(None, "tp"),
        P(None, "tp"),
        P(),
        P(),
        P(),
        P(),
        P(),
        P("ep", None, "tp"),
        P("ep", None, "tp"),
        P("ep", "tp", None),
        P("ep", None),
    )
    out_specs = (
        P("ep", None),
        P("ep", None),
        P("ep", "tp"),
        P("ep", "tp"),
        P("ep", "tp"),
        P("ep", "tp"),
        P("ep"),
        P(),
        P(),
        P("ep"),
        P("ep", None),
        P("ep", None, "tp"),
        P("ep", None, "tp"),
        P("ep", "tp", None),
    )
    return jax.shard_map(
        per_device, mesh=mesh, in_specs=in_specs, out_specs=out_specs, check_vma=False
    )
```

```python
import math

import jax
import jax.numpy as jnp
from jax import lax
from jax.experimental import pallas as pl
from jax.experimental.pallas import tpu as pltpu
from jax.sharding import PartitionSpec as P

EPSILON = 1e-06
THETA = 1000000.0
MASKED = -1e30
PROJECT_FIRST, PROJECT_LAST = 100.0, 1.0
HALVES_FIRST, HALVES_LATER = 0.1, 100.0
BF = jnp.bfloat16
F32 = jnp.float32
COLS = (((1,), (1,)), ((), ()))
ROWS = (((0,), (0,)), ((), ()))


def norm_rate(value_rows):
    return lax.rsqrt(jnp.mean(value_rows * value_rows, axis=-1, keepdims=True) + EPSILON)


def norm_back(value_rows, rate, gain, upstream):
    scaled = upstream * gain
    inner = jnp.mean(scaled * value_rows, axis=-1, keepdims=True)
    return rate * scaled - value_rows * (rate * rate * rate) * inner


def rope_tables(doc_ids, head_dim):
    half_dim = head_dim // 2
    starts = jnp.sum((doc_ids[None, :] < doc_ids[:, None]).astype(jnp.int32), axis=1)
    places = jnp.arange(doc_ids.shape[0], dtype=jnp.int32) - starts
    inverse = THETA ** (-jnp.arange(half_dim, dtype=F32) * 2.0 / head_dim)
    angles = places.astype(F32)[:, None] * inverse[None, :]
    cosine, sine = jnp.cos(angles), jnp.sin(angles)
    return (
        jnp.concatenate([cosine, cosine], axis=1),
        jnp.concatenate([-sine, sine], axis=1),
    )


def fixed(shape):
    return pl.BlockSpec(shape, lambda i: (0,) * len(shape))


def cost(flops, bytes_accessed, weight=1.0):
    return pl.CostEstimate(
        flops=int(flops * weight) + 1, bytes_accessed=int(bytes_accessed * weight) + 1, transcendentals=0
    )


def joined(*groups):
    flat = lax.optimization_barrier(tuple(value for group in groups for value in group))
    result, at = [], 0
    for group in groups:
        result.append(list(flat[at : at + len(group)]))
        at += len(group)
    return result


def params():
    return pltpu.CompilerParams(vmem_limit_bytes=60 * 2**20)


def turn(rows, cos, sin):
    return rows * cos + pltpu.roll(rows, rows.shape[1] // 2, 1) * sin


def turn_back(rows, cos, sin):
    return rows * cos - pltpu.roll(rows, rows.shape[1] // 2, 1) * sin


def attend_kernel(
    head_dim, scale,
    tokens_ref, gain_ref, query_ref, key_ref, value_ref, column_ref, row_ref, cos_ref, sin_ref, query_gain_ref, key_gain_ref,
    normed_ref, rate_ref, heads_ref, query_raw_ref, query_low_ref, probs_ref, key_raw_ref, key_low_ref, value_low_ref,
    bias_ref, value_turned_ref,
):
    length = tokens_ref.shape[0]

    @pl.when(pl.program_id(0) == 0)
    def _():
        wide = tokens_ref[...].astype(F32)
        rate = norm_rate(wide)
        rate_ref[...] = jnp.broadcast_to(rate, rate_ref.shape)
        normed_ref[...] = (wide * rate * gain_ref[...]).astype(BF)
        keys = jnp.dot(normed_ref[...], key_ref[...], preferred_element_type=F32)
        key_raw_ref[...] = keys
        key_low_ref[...] = turn(
            keys * norm_rate(keys) * key_gain_ref[...], cos_ref[...], sin_ref[...]
        ).astype(BF)
        values = jnp.dot(normed_ref[...], value_ref[...], preferred_element_type=F32)
        value_low_ref[...] = values.astype(BF)
        value_turned_ref[...] = values.T.astype(BF)
        key_place = lax.broadcasted_iota(jnp.int32, (length, length), 0)
        query_place = lax.broadcasted_iota(jnp.int32, (length, length), 1)
        allowed = (key_place <= query_place) & (column_ref[...] == row_ref[...])
        bias_ref[...] = jnp.where(allowed, 0.0, MASKED)

    query_raw = jnp.dot(normed_ref[...], query_ref[...], preferred_element_type=F32)
    query_raw_ref[...] = query_raw
    for head in range(query_raw.shape[1] // head_dim):
        span = slice(head * head_dim, (head + 1) * head_dim)
        query = query_raw[:, span]
        query_low = turn(
            query * norm_rate(query) * query_gain_ref[...], cos_ref[...], sin_ref[...]
        ).astype(BF)
        query_low_ref[:, span] = query_low
        scores = (
            lax.dot_general(key_low_ref[...], query_low, COLS, preferred_element_type=F32) * scale
            + bias_ref[...]
        )
        exps = jnp.exp(scores - jnp.max(scores, axis=0, keepdims=True))
        probs = exps * (1.0 / jnp.sum(exps, axis=0, keepdims=True))
        probs_ref[head] = probs
        mixed = jnp.dot(value_turned_ref[...], probs.astype(BF), preferred_element_type=F32)
        heads_ref[:, span] = mixed.T.astype(BF)


def attend(
    tokens, doc_ids, query_weight, key_matrix, value_matrix, attn_gain, query_gain, key_gain, cos, sin, weight=1.0
):
    length, width = tokens.shape
    head_dim = query_gain.shape[0]
    cols = query_weight.shape[1]
    step = min(2 * head_dim, cols)
    heads = cols // head_dim
    narrow = pl.BlockSpec((length, step), lambda i: (0, i))
    single = fixed((length, head_dim))
    return pl.pallas_call(
        lambda *refs: attend_kernel(head_dim, 1.0 / math.sqrt(head_dim), *refs),
        grid=(cols // step,),
        in_specs=[
            fixed((length, width)), fixed((1, width)),
            pl.BlockSpec((width, step), lambda i: (0, i)),
            fixed((width, head_dim)), fixed((width, head_dim)),
            fixed((length, 1)), fixed((1, length)), single, single,
            fixed((1, head_dim)), fixed((1, head_dim)),
        ],
        out_specs=[
            fixed((length, width)), single, narrow, narrow, narrow,
            pl.BlockSpec((step // head_dim, length, length), lambda i: (i, 0, 0)),
            single, single, single,
        ],
        out_shape=[
            jax.ShapeDtypeStruct((length, width), BF),
            jax.ShapeDtypeStruct((length, head_dim), F32),
            jax.ShapeDtypeStruct((length, cols), BF),
            jax.ShapeDtypeStruct((length, cols), F32),
            jax.ShapeDtypeStruct((length, cols), BF),
            jax.ShapeDtypeStruct((heads, length, length), F32),
            jax.ShapeDtypeStruct((length, head_dim), F32),
            jax.ShapeDtypeStruct((length, head_dim), BF),
            jax.ShapeDtypeStruct((length, head_dim), BF),
        ],
        scratch_shapes=[pltpu.VMEM((length, length), F32), pltpu.VMEM((head_dim, length), BF)],
        compiler_params=params(),
        cost_estimate=cost(2 * length * width * cols, 2 * width * cols, weight),
    )(
        tokens, attn_gain[None, :], query_weight, key_matrix, value_matrix,
        doc_ids[:, None], doc_ids[None, :], cos, sin, query_gain[None, :], key_gain[None, :],
    )


def norm_parts(raw, gain, upstream):
    rate = norm_rate(raw)
    gain_grad = jnp.sum(upstream * raw * rate, axis=0, keepdims=True)
    return norm_back(raw, rate, gain, upstream), gain_grad


def gather_rows(blocks, *whole_refs):
    count, me = len(blocks), lax.axis_index("tp")
    size = blocks[0].shape[0]
    for shift, block in enumerate(blocks):
        start = pl.multiple_of((me + count - shift) % count * size, size)
        first = 0
        for whole_ref in whole_refs:
            last = first + whole_ref.shape[1]
            whole_ref[pl.ds(start, size), :] = block[:, first:last]
            first = last


def attend_back_kernel(
    count, head_dim, scale, *refs
):
    blocks = refs[:count]
    (
        out_ref, query_raw_ref, query_low_ref, probs_ref, key_raw_ref, key_low_ref, value_low_ref, cos_ref, sin_ref, query_gain_ref, key_gain_ref,
        branch_ref, logit_ref, grads_ref, gains_ref,
        key_turned_ref, key_sum, value_sum,
    ) = refs[count:]
    step = pl.program_id(0)
    cols = query_raw_ref.shape[1]

    @pl.when(step == 0)
    def _():
        gather_rows(blocks, branch_ref, logit_ref)
        key_turned_ref[...] = key_low_ref[...].astype(F32).T.astype(BF)
        key_sum[...] = jnp.zeros_like(key_sum)
        value_sum[...] = jnp.zeros_like(value_sum)
        gains_ref[...] = jnp.zeros_like(gains_ref)

    heads_grad = jnp.dot(branch_ref[...], out_ref[...], preferred_element_type=F32).astype(BF)
    cos, sin = cos_ref[...], sin_ref[...]
    for head in range(cols // head_dim):
        span = slice(head * head_dim, (head + 1) * head_dim)
        upstream = heads_grad[:, span]
        probs = probs_ref[head]
        prob_grad = lax.dot_general(
            value_low_ref[...], upstream, COLS, preferred_element_type=F32
        )
        delta = jnp.sum(probs * prob_grad, axis=0, keepdims=True)
        score_grad = (probs * (prob_grad - delta)).astype(BF)
        value_sum[...] += jnp.dot(probs.astype(BF), upstream, preferred_element_type=F32)
        key_sum[...] += jnp.dot(score_grad, query_low_ref[:, span], preferred_element_type=F32)
        turned = jnp.dot(key_turned_ref[...], score_grad, preferred_element_type=F32)
        query_back = (turned.T * scale).astype(BF).astype(F32)
        grad, gain = norm_parts(
            query_raw_ref[:, span], query_gain_ref[...], turn_back(query_back, cos, sin)
        )
        gains_ref[0:1, :] += gain
        start = pl.multiple_of(step * cols + head * head_dim, head_dim)
        grads_ref[:, pl.ds(start, head_dim)] = grad.astype(BF)

    @pl.when(step == pl.num_programs(0) - 1)
    def _():
        key_back = (key_sum[...] * scale).astype(BF).astype(F32)
        grad, gain = norm_parts(key_raw_ref[...], key_gain_ref[...], turn_back(key_back, cos, sin))
        gains_ref[1:2, :] += gain
        last = grads_ref.shape[1]
        grads_ref[:, last - 2 * head_dim : last - head_dim] = grad.astype(BF)
        grads_ref[:, last - head_dim :] = value_sum[...].astype(BF)


def attend_back(
    blocks, output_weight, query_raw, query_low, probs, key_raw, key_low, value_low, cos, sin, query_gain, key_gain, weight=0.1
):
    count, (size, wide), width = len(blocks), blocks[0].shape, output_weight.shape[0]
    length, cols = query_raw.shape
    head_dim = query_gain.shape[0]
    step = min(8 * head_dim, cols)
    single = fixed((length, head_dim))
    narrow = pl.BlockSpec((length, step), lambda i: (0, i))
    return pl.pallas_call(
        lambda *refs: attend_back_kernel(count, head_dim, 1.0 / math.sqrt(head_dim), *refs),
        grid=(cols // step,),
        in_specs=[fixed((size, wide))] * count
        + [
            pl.BlockSpec((width, step), lambda i: (0, i)), narrow, narrow,
            pl.BlockSpec((step // head_dim, length, length), lambda i: (i, 0, 0)),
            single, single, single, single, single, fixed((1, head_dim)), fixed((1, head_dim)),
        ],
        out_specs=[
            fixed((length, width)), fixed((length, wide - width)),
            fixed((length, cols + 2 * head_dim)), fixed((8, head_dim)),
        ],
        out_shape=[
            jax.ShapeDtypeStruct((length, width), BF),
            jax.ShapeDtypeStruct((length, wide - width), BF),
            jax.ShapeDtypeStruct((length, cols + 2 * head_dim), BF),
            jax.ShapeDtypeStruct((8, head_dim), F32),
        ],
        scratch_shapes=[
            pltpu.VMEM((head_dim, length), BF),
            pltpu.VMEM((length, head_dim), F32),
            pltpu.VMEM((length, head_dim), F32),
        ],
        compiler_params=params(),
        cost_estimate=cost(2 * length * width * cols, 2 * width * cols, weight),
    )(
        *blocks, output_weight, query_raw, query_low, probs, key_raw, key_low, value_low, cos, sin,
        query_gain[None, :], key_gain[None, :],
    )


def route_kernel(
    capacity, tp_count,
    routes_ref, turned_ref, rows_ref,
    mask_ref, turned_mask_ref, routed_ref, sent_ref,
    places_ref,
):
    length, top_count = routes_ref.shape
    experts, slots = routed_ref.shape[1], mask_ref.shape[1]
    owners = slots // capacity
    step, tile = pl.program_id(0), turned_mask_ref.shape[0]
    me = lax.axis_index("tp")

    def iota(shape, axis):
        return lax.broadcasted_iota(jnp.int32, shape, axis)

    def low(flags):
        return flags.astype(F32).astype(BF)

    @pl.when(step == 0)
    def _():
        expert = iota((length, experts), 1)
        routed = jnp.zeros((length, experts), F32)
        turned = jnp.zeros((experts, length), F32)
        for k in range(top_count):
            routed += (routes_ref[:, k : k + 1] == expert).astype(F32)
            turned += (turned_ref[k : k + 1, :] == iota((experts, length), 0)).astype(F32)
        routed_ref[...] = routed.astype(BF)
        own = jnp.dot(
            routed_ref[...],
            low(iota((experts, owners), 0) == iota((experts, owners), 1) * tp_count + me),
            preferred_element_type=F32,
        )
        earlier = low(iota((length, length), 0) > iota((length, length), 1))
        rank = jnp.dot(earlier, own.astype(BF), preferred_element_type=F32)
        places = jnp.where(own > 0.5, rank, -1.0).astype(BF)
        slot = iota((owners, slots), 1)
        wide = jnp.dot(
            places, low(lax.div(slot, capacity) == iota((owners, slots), 0)), preferred_element_type=F32
        )
        mask_ref[...] = low(wide == lax.rem(iota((1, slots), 1), capacity).astype(F32))
        own_turned = jnp.dot(
            low(iota((owners, experts), 1) == iota((owners, experts), 0) * tp_count + me),
            turned.astype(BF),
            preferred_element_type=F32,
        )
        later = low(iota((length, length), 0) < iota((length, length), 1))
        rank_turned = jnp.dot(own_turned.astype(BF), later, preferred_element_type=F32)
        places_ref[...] = jnp.where(own_turned > 0.5, rank_turned, -1.0).astype(BF)

    slot = iota((tile, owners), 0) + step * tile
    wide = jnp.dot(
        low(lax.div(slot, capacity) == iota((tile, owners), 1)), places_ref[...], preferred_element_type=F32
    )
    mask = low(wide == lax.rem(iota((tile, 1), 0) + step * tile, capacity).astype(F32))
    turned_mask_ref[...] = mask
    width = rows_ref.shape[1]
    sent_ref[:, :width] = jnp.dot(mask, rows_ref[...], preferred_element_type=F32).astype(BF)
    sent_ref[:, width:] = jnp.dot(mask, routed_ref[...], preferred_element_type=F32).astype(BF)


def route(routes, rows, experts, capacity, ep_count, tp_count, weight=1.0):
    (length, top_count), width = routes.shape, rows.shape[1]
    slots = ep_count * capacity
    tile = min(256, slots)
    return pl.pallas_call(
        lambda *refs: route_kernel(capacity, tp_count, *refs),
        grid=(slots // tile,),
        in_specs=[fixed((length, top_count)), fixed((top_count, length)), fixed((length, width))],
        out_specs=[
            fixed((length, slots)),
            pl.BlockSpec((tile, length), lambda i: (i, 0)),
            fixed((length, experts)),
            pl.BlockSpec((tile, width + experts), lambda i: (i, 0)),
        ],
        out_shape=[
            jax.ShapeDtypeStruct((length, slots), BF),
            jax.ShapeDtypeStruct((slots, length), BF),
            jax.ShapeDtypeStruct((length, experts), BF),
            pltpu.HBM((slots, width + experts), BF),
        ],
        scratch_shapes=[pltpu.VMEM((ep_count, length), BF)],
        compiler_params=params(),
        cost_estimate=cost(2 * length * slots * width, 2 * slots * width, weight),
    )(routes, routes.T, rows)


def gate_kernel(capacity, tp_count, rows_ref, router_ref, routed_ref, mask_ref, probs_ref, weight_ref):
    experts, slots = routed_ref.shape[1], mask_ref.shape[1]
    owners = slots // capacity
    me = lax.axis_index("tp")

    def iota(shape, axis):
        return lax.broadcasted_iota(jnp.int32, shape, axis)

    logits = jnp.dot(rows_ref[...], router_ref[...], preferred_element_type=F32)
    logits = jnp.where(routed_ref[...].astype(F32) > 0.5, logits, MASKED)
    exps = jnp.exp(logits - jnp.max(logits, axis=1, keepdims=True))
    probs = exps / jnp.sum(exps, axis=1, keepdims=True)
    probs_ref[...] = probs
    spread = (
        iota((experts, slots), 0) == lax.div(iota((experts, slots), 1), capacity) * tp_count + me
    )
    weights = jnp.dot(
        probs.astype(BF), spread.astype(F32).astype(BF), preferred_element_type=F32
    )
    weight_ref[...] = weights.astype(BF) * mask_ref[...]


def gate_weights(rows, router_weight, routed, mask, capacity, ep_count, tp_count, weight=1.0):
    length, slots = mask.shape
    return pl.pallas_call(
        lambda *refs: gate_kernel(capacity, tp_count, *refs),
        out_shape=[
            jax.ShapeDtypeStruct(routed.shape, F32),
            jax.ShapeDtypeStruct((length, slots), BF),
        ],
        compiler_params=params(),
        cost_estimate=cost(2 * length * routed.shape[1] * (rows.shape[1] + slots), 4 * length * slots, weight),
    )(rows, router_weight, routed, mask)


def fill_kernel(count, *refs):
    blocks, (mask_ref, sent_ref, whole_ref) = refs[:count], refs[count:]

    @pl.when(pl.program_id(0) == 0)
    def _():
        gather_rows(blocks, whole_ref)

    sent_ref[...] = jnp.dot(mask_ref[...], whole_ref[...], preferred_element_type=F32).astype(BF)


def fill(blocks, turned_mask, weight=0.1):
    count, (size, width) = len(blocks), blocks[0].shape
    slots, length = turned_mask.shape
    tile = min(512, slots)
    return pl.pallas_call(
        lambda *refs: fill_kernel(count, *refs),
        grid=(slots // tile,),
        in_specs=[fixed((size, width))] * count + [pl.BlockSpec((tile, length), lambda i: (i, 0))],
        out_specs=[pl.BlockSpec((tile, width), lambda i: (i, 0)), fixed((length, width))],
        out_shape=[
            pltpu.HBM((slots, width), BF),
            jax.ShapeDtypeStruct((length, width), BF),
        ],
        compiler_params=params(),
        cost_estimate=cost(2 * length * slots * width, 2 * slots * width, weight),
    )(*blocks, turned_mask)


def after(value, *earlier):
    return lax.optimization_barrier((value,) + earlier)[0]


def ring(count, shift):
    return [(i, (i + shift) % count) for i in range(count)]


def row_block(value_rows, index, count):
    size = value_rows.shape[0] // count
    return lax.dynamic_slice_in_dim(value_rows, index * size, size, 0)


def tp_spread(block):
    count = lax.axis_size("tp")
    return [block] + [lax.ppermute(block, "tp", ring(count, shift)) for shift in range(1, count)]


def tp_join(blocks):
    count, me = lax.axis_size("tp"), lax.axis_index("tp")
    whole = jnp.zeros((count,) + blocks[0].shape, blocks[0].dtype)
    for shift, block in enumerate(blocks):
        whole = lax.dynamic_update_index_in_dim(whole, block, (me - shift) % count, 0)
    return whole.reshape((-1,) + blocks[0].shape[1:])


def tp_sum_blocks(blocks):
    count = lax.axis_size("tp")
    total = blocks[0].astype(F32)
    for shift in range(1, count):
        total = total + lax.ppermute(blocks[shift], "tp", ring(count, shift)).astype(F32)
    return total


def project_kernel(count, spans, left_ref, *refs):
    rights, refs = refs[: len(spans)], refs[len(spans) :]
    outs, held = refs[-count - 1 : -1], refs[-1]
    me = lax.axis_index("tp")
    size = left_ref.shape[0] // count
    for right_ref, (first, last) in zip(rights, spans):
        got = lax.dot_general(
            left_ref[:, first:last], right_ref[...], COLS, preferred_element_type=F32
        )
        if first == 0:
            held[...] = got
        else:
            held[...] += got
    for shift in range(count):
        start = pl.multiple_of((me + shift) % count * size, size)
        outs[shift][...] = held[pl.ds(start, size), :].astype(BF)
    if len(refs) > count + 1:
        rows_ref, rate_ref, gain_ref = refs[:3]
        gain_ref[...] = jnp.sum(
            held[...] * (rows_ref[...].astype(F32) * rate_ref[:, :1]), axis=0, keepdims=True
        )


def project(left, rights, rows=None, rate=None, tile=1024, weight=1.0):
    count = lax.axis_size("tp")
    length, width = left.shape[0], rights[0].shape[0]
    tile = min(tile, width)
    spans, first = [], 0
    for right in rights:
        spans.append((first, first + right.shape[1]))
        first += right.shape[1]
    size = length // count
    in_specs = [fixed(left.shape)]
    in_specs += [pl.BlockSpec((tile, right.shape[1]), lambda i: (i, 0)) for right in rights]
    out_specs = [pl.BlockSpec((size, tile), lambda i: (0, i))] * count
    out_shape = [jax.ShapeDtypeStruct((size, width), BF)] * count
    more = []
    if rows is not None:
        more = [rows, rate]
        in_specs += [pl.BlockSpec((length, tile), lambda i: (0, i)), fixed(rate.shape)]
        out_specs = [pl.BlockSpec((1, tile), lambda i: (0, i))] + out_specs
        out_shape = [jax.ShapeDtypeStruct((1, width), F32)] + out_shape
    return pl.pallas_call(
        lambda *refs: project_kernel(count, spans, *refs),
        grid=(width // tile,),
        in_specs=in_specs,
        out_specs=out_specs,
        out_shape=out_shape,
        scratch_shapes=[pltpu.VMEM((length, tile), F32)],
        compiler_params=params(),
        cost_estimate=cost(2 * length * first * width, 2 * first * width, weight),
    )(left, *rights, *more)


def expert_kernel(
    width, rows_ref, grads_ref, *refs
):
    count = (len(refs) - 7) // 2
    sources = [refs[:count], refs[count : 2 * count]]
    back_ref, act_ref, gate_back_ref, up_back_ref, *held, sems = refs[2 * count :]
    size = sources[0][0].shape[0]

    def loads(which):
        return [
            pltpu.make_async_copy(
                source, held[which].at[pl.ds(part * size, size), :], sems.at[which, part]
            )
            for part, source in enumerate(sources[which])
        ]

    first = pl.program_id(0) == 0

    @pl.when(first)
    def _():
        for which in range(2):
            for load in loads(which):
                load.start()
        for load in loads(0):
            load.wait()

    rows = rows_ref[...]
    gate_val = lax.dot_general(rows, held[0][...], COLS, preferred_element_type=F32)

    @pl.when(first)
    def _():
        for load in loads(1):
            load.wait()

    up_val = lax.dot_general(rows, held[1][...], COLS, preferred_element_type=F32)

    act_grad = grads_ref[...]
    gate_sig = jax.nn.sigmoid(gate_val)
    gate_act = gate_val * gate_sig
    act_low = (gate_act * up_val).astype(BF)
    act_ref[...] = act_low
    gate_back = (act_grad * up_val * gate_sig * (1.0 + gate_val * (1.0 - gate_sig))).astype(BF)
    up_back = (act_grad * gate_act).astype(BF)
    gate_back_ref[...] = gate_back
    up_back_ref[...] = up_back
    slot_grad = jnp.sum(act_low.astype(F32) * act_grad, axis=1, keepdims=True)
    back_ref[:, width:] = jnp.broadcast_to(
        slot_grad, (rows.shape[0], back_ref.shape[1] - width)
    ).astype(BF)
    back_ref[:, :width] = (
        jnp.dot(gate_back, held[0][...], preferred_element_type=F32)
        + jnp.dot(up_back, held[1][...], preferred_element_type=F32)
    ).astype(BF)


def hidden_kernel(rows_ref, *refs):
    blocks, out_ref = refs[:-1], refs[-1]
    size = blocks[0].shape[0]
    for part, block in enumerate(blocks):
        out_ref[:, part * size : (part + 1) * size] = lax.dot_general(
            rows_ref[...], block[...], COLS, preferred_element_type=F32
        )


def hidden_grads(rows, downs, tile=256, weight=10.0):
    slots, (size, width) = rows.shape[0], downs[0].shape
    tile = min(tile, slots)
    return pl.pallas_call(
        hidden_kernel,
        grid=(slots // tile,),
        in_specs=[pl.BlockSpec((tile, width), lambda i: (i, 0))] + [fixed((size, width))] * len(downs),
        out_specs=pl.BlockSpec((tile, size * len(downs)), lambda i: (i, 0)),
        out_shape=pltpu.HBM((slots, size * len(downs)), F32),
        compiler_params=params(),
        cost_estimate=cost(2 * slots * width * size * len(downs), 2 * slots * width, weight),
    )(rows, *downs)


def expert_pass(rows_in, act_grad, gates, ups, extra, tile=256, weight=1.0):
    slots, width = rows_in.shape
    tile = min(tile, slots)
    hidden = len(gates) * gates[0].shape[0]
    tall = pl.BlockSpec((tile, width), lambda i: (i, 0))
    narrow = pl.BlockSpec((tile, hidden), lambda i: (i, 0))
    low = jax.ShapeDtypeStruct((slots, hidden), BF)
    return pl.pallas_call(
        lambda *refs: expert_kernel(width, *refs),
        grid=(slots // tile,),
        in_specs=[tall, narrow] + [pl.BlockSpec(memory_space=pl.ANY)] * (2 * len(gates)),
        out_specs=[pl.BlockSpec((tile, width + extra), lambda i: (i, 0)), narrow, narrow, narrow],
        out_shape=[pltpu.HBM((slots, width + extra), BF), low, low, low],
        scratch_shapes=[pltpu.VMEM((hidden, width), BF)] * 2
        + [pltpu.SemaphoreType.DMA((2, len(gates)))],
        compiler_params=params(),
        cost_estimate=cost(8 * slots * width * hidden, 6 * slots * width + 6 * width * hidden, weight),
    )(rows_in, act_grad, *gates, *ups)


def place_kernel(count, *refs):
    ins, out_ref = refs[:count], refs[count]
    step = pl.program_id(0)
    for shift in range(count):

        @pl.when(step == shift)
        def _():
            out_ref[0] = ins[shift][...].astype(out_ref.dtype)


def place_blocks(blocks, direction, dtype, tile, weight=1.0):
    count, me = len(blocks), lax.axis_index("tp")
    rows, cols = blocks[0].shape
    steps = rows // tile

    def held(shift):
        return lambda s, t, me_ref: (jnp.where(s < shift, 0, jnp.where(s > shift, steps - 1, t)), 0)

    return pl.pallas_call(
        lambda me_ref, *refs: place_kernel(count, *refs),
        grid_spec=pltpu.PrefetchScalarGridSpec(
            num_scalar_prefetch=1,
            grid=(count, steps),
            in_specs=[pl.BlockSpec((tile, cols), held(shift)) for shift in range(count)],
            out_specs=pl.BlockSpec(
                (1, tile, cols), lambda s, t, me_ref: ((me_ref[0] + direction * s + count) % count, t, 0)
            ),
        ),
        out_shape=jax.ShapeDtypeStruct((count, rows, cols), dtype),
        compiler_params=params(),
        cost_estimate=cost(0, count * rows * cols * (2 + jnp.dtype(dtype).itemsize), weight),
    )(me.astype(jnp.int32).reshape(1), *blocks)


def pull_slices(weights, picks):
    count, me = lax.axis_size("tp"), lax.axis_index("tp")
    return [
        lax.dynamic_index_in_dim(weights[which], (me + shift) % count, 0, keepdims=False)
        for which, shift in picks
    ]


def shift_blocks(blocks, shifts):
    count = lax.axis_size("tp")
    return [
        lax.ppermute(block, "tp", ring(count, shift)) for block, shift in zip(blocks, shifts)
    ]


def push_blocks(grad, shifts=None):
    count = lax.axis_size("tp")
    size = grad.shape[0] // count
    blocks = []
    for shift in range(count) if shifts is None else shifts:
        block = grad[shift * size : (shift + 1) * size]
        blocks.append(lax.ppermute(block, "tp", ring(count, -shift)) if shift else block)
    return blocks


def place_experts(blocks):
    return place_blocks(blocks, 1, F32, blocks[0].shape[0])


def ep_exchange(rows):
    return lax.all_to_all(rows, "ep", 0, 0, tiled=True)


def wgrad_kernel(share, spans, *refs):
    count = len(spans)
    lefts, rights, (keep_ref, send_ref, held) = refs[:count], refs[count : 2 * count], refs[2 * count :]
    core = lax.axis_index("ep") % 2
    for left_ref, right_ref, (first, size) in zip(lefts, rights, spans):
        held[:, first : first + size] = lax.dot_general(
            left_ref[...], right_ref[...], ROWS, preferred_element_type=F32
        )
    split_cores(share, core, held, keep_ref, send_ref)


def split_cores(share, core, held, keep_ref, send_ref):
    for chip in range(held.shape[0] // (2 * share)):
        kept = pl.multiple_of((2 * chip + core) * share, share)
        sent = pl.multiple_of((2 * chip + 1 - core) * share, share)
        keep_ref[chip * share : (chip + 1) * share, :] = held[pl.ds(kept, share), :].astype(BF)
        send_ref[chip * share : (chip + 1) * share, :] = held[pl.ds(sent, share), :].astype(BF)


def grad_halves(pairs, tile=1024, weight=1.0):
    count = lax.axis_size("ep")
    length, width = pairs[0][0].shape
    share = width // count
    tile = min(tile, width)
    spans, cols = [], 0
    for _, right in pairs:
        spans.append((cols, right.shape[1]))
        cols += right.shape[1]
    half = pl.BlockSpec((tile // 2, cols), lambda i: (i, 0))
    return pl.pallas_call(
        lambda *refs: wgrad_kernel(share, spans, *refs),
        grid=(width // tile,),
        in_specs=[pl.BlockSpec((length, tile), lambda i: (0, i))] * len(pairs)
        + [pl.BlockSpec(right.shape, lambda i: (0, 0)) for _, right in pairs],
        out_specs=[half, half],
        out_shape=[pltpu.HBM((width // 2, cols), BF)] * 2,
        scratch_shapes=[pltpu.VMEM((tile, cols), F32)],
        compiler_params=params(),
        cost_estimate=cost(2 * length * width * cols, 3 * width * cols, weight),
    )(*[left for left, _ in pairs], *[right for _, right in pairs])


def swap_cores(value):
    return lax.ppermute(value, "ep", [(i, i ^ 1) for i in range(lax.axis_size("ep"))])


def pair_kernel(share, first_keep, first_got, second_keep, second_got, extra_ref, out_ref):
    for chip in range(out_ref.shape[0]):
        rows, row = slice(chip * share, (chip + 1) * share), 0
        for keep_ref, got_ref in ((first_keep, first_got), (second_keep, second_got)):
            for column in range(0, keep_ref.shape[1], 128):
                span = slice(column, column + 128)
                both = keep_ref[rows, span].astype(F32) + got_ref[rows, span].astype(F32)
                out_ref[chip, row : row + share, :] = both.astype(BF)
                row += share
        out_ref[chip, row:, :] = extra_ref[chip]


def pair_sums(pairs, extra, weight=1.0):
    chips = extra.shape[0]
    share = pairs[0][0].shape[0] // chips
    step = min(4, chips)
    blocks = [pl.BlockSpec((step * share, keep.shape[1]), lambda i: (i, 0)) for keep, _ in pairs for _ in range(2)]
    rows = sum(keep.shape[1] // 128 * share for keep, _ in pairs) + extra.shape[1]
    return pl.pallas_call(
        lambda *refs: pair_kernel(share, *refs),
        grid=(chips // step,),
        in_specs=blocks + [pl.BlockSpec((step,) + extra.shape[1:], lambda i: (i, 0, 0))],
        out_specs=pl.BlockSpec((step, rows, 128), lambda i: (i, 0, 0)),
        out_shape=pltpu.HBM((chips, rows, 128), BF),
        compiler_params=params(),
        cost_estimate=cost(0, 8 * chips * rows * 128, weight),
    )(*[value for pair in pairs for value in pair], extra)


def chip_kernel(widths, parts_ref, *outs):
    share, row = outs[0].shape[0], 0
    for out_ref, width in zip(outs, widths):
        for column in range(0, width, 128):
            part = parts_ref[:, row : row + share, :].astype(F32)
            out_ref[:, column : column + 128] = jnp.sum(part, axis=0)
            row += share
    outs[-1][...] = jnp.sum(parts_ref[:, row:, :].astype(F32), axis=0)


def chip_sums(parts, widths, share, weight=1.0):
    rest = parts.shape[1] - sum(widths) // 128 * share
    return pl.pallas_call(
        lambda *refs: chip_kernel(widths, *refs),
        out_shape=[jax.ShapeDtypeStruct((share, width), F32) for width in widths]
        + [jax.ShapeDtypeStruct((rest, 128), F32)],
        compiler_params=params(),
        cost_estimate=cost(0, 2 * parts.size, weight),
    )(parts)


def chip_exchange(parts):
    count = lax.axis_size("ep")
    if count == 2:
        return parts
    groups = [list(range(side, count, 2)) for side in range(2)]
    return lax.all_to_all(parts, "ep", 0, 0, axis_index_groups=groups, tiled=True)


def core_sum(extra):
    core, many = lax.axis_index("ep") % 2, extra.shape[1]
    extra = extra.reshape(-1, 2, many)
    total = lax.dynamic_index_in_dim(extra, core, 1, keepdims=False)
    total += swap_cores(lax.dynamic_index_in_dim(extra, 1 - core, 1, keepdims=False))
    total = total.reshape(total.shape[0], -1, 128)
    high = total.astype(BF)
    low = (total - high.astype(F32)).astype(BF)
    rows = jnp.concatenate([high, low], axis=1)
    return jnp.pad(rows, ((0, 0), (0, -rows.shape[1] % 8), (0, 0)))


def combine_kernel(count, capacity, width, weight_ref, mask_ref, rows_ref, *refs):
    outs, held = refs[:-1], refs[-1]
    me = lax.axis_index("tp")
    size = weight_ref.shape[0] // count
    shape = (rows_ref.shape[0], rows_ref.shape[1] - width)
    owner = lax.div(lax.broadcasted_iota(jnp.int32, shape, 0), capacity)
    named = owner * count + me == lax.broadcasted_iota(jnp.int32, shape, 1)
    held[:, :width] = jnp.dot(weight_ref[...], rows_ref[:, :width], preferred_element_type=F32)
    held[:, width:] = jnp.dot(
        mask_ref[...], rows_ref[:, width:] * named.astype(F32).astype(BF), preferred_element_type=F32
    )
    for shift in range(count):
        start = pl.multiple_of((me + shift) % count * size, size)
        outs[shift][...] = held[pl.ds(start, size), :].astype(BF)


def combine(weights, mask, rows, width, capacity, weight=0.0):
    count = lax.axis_size("tp")
    length, wide = weights.shape[0], rows.shape[1]
    return pl.pallas_call(
        lambda *refs: combine_kernel(count, capacity, width, *refs),
        out_shape=[jax.ShapeDtypeStruct((length // count, wide), BF)] * count,
        scratch_shapes=[pltpu.VMEM((length, wide), F32)],
        compiler_params=params(),
        cost_estimate=cost(2 * length * rows.shape[0] * wide, 2 * rows.shape[0] * wide, weight),
    )(weights, mask, rows)


def mix_kernel(count, weight_ref, rows_ref, *refs):
    outs, held = refs[:-1], refs[-1]
    me = lax.axis_index("tp")
    size = weight_ref.shape[0] // count
    held[...] = jnp.dot(weight_ref[...], rows_ref[...], preferred_element_type=F32)
    for shift in range(count):
        start = pl.multiple_of((me + shift) % count * size, size)
        outs[shift][...] = held[pl.ds(start, size), :].astype(BF)


def mix(weights, rows, tile=512, weight=10.0):
    count = lax.axis_size("tp")
    (length, slots), width = weights.shape, rows.shape[1]
    tile = min(tile, width)
    return pl.pallas_call(
        lambda *refs: mix_kernel(count, *refs),
        grid=(width // tile,),
        in_specs=[fixed((length, slots)), pl.BlockSpec((slots, tile), lambda i: (0, i))],
        out_specs=[pl.BlockSpec((length // count, tile), lambda i: (0, i))] * count,
        out_shape=[jax.ShapeDtypeStruct((length // count, width), BF)] * count,
        scratch_shapes=[pltpu.VMEM((length, tile), F32)],
        compiler_params=params(),
        cost_estimate=cost(2 * length * slots * width, 2 * slots * width, weight),
    )(weights, rows)


def tp_sum(value):
    count, total = lax.axis_size("tp"), value
    for shift in range(1, count):
        total = total + lax.ppermute(value, "tp", ring(count, shift))
    return total


def per_device(
    tokens,
    doc_ids,
    routes,
    query_weight,
    key_matrix,
    value_matrix,
    output_weight,
    attn_gain,
    query_gain,
    key_gain,
    mlp_gain,
    router_weight,
    gate_weight,
    up_weight,
    down_weight,
    cotangent,
):
    length, width = tokens.shape
    head_dim = query_gain.shape[0]
    total_experts = router_weight.shape[1]
    top_count = routes.shape[1]
    ep_count, tp_count = lax.axis_size("ep"), lax.axis_size("tp")
    ep_index, tp_index = lax.axis_index("ep"), lax.axis_index("tp")
    capacity = length * top_count * 4 // (3 * total_experts)
    slots = ep_count * capacity

    near, far = (1, tp_count - 1), range(2, tp_count - 1)
    weights = (jnp.swapaxes(gate_weight, 1, 2), jnp.swapaxes(up_weight, 1, 2), down_weight)
    near_gates_out = pull_slices(weights, [(0, shift) for shift in near])
    far_gates_out = pull_slices(weights, [(0, shift) for shift in far])
    near_ups_out = pull_slices(weights, [(1, shift) for shift in near])
    far_ups_out = pull_slices(weights, [(1, shift) for shift in far])
    near_downs_out = pull_slices(weights, [(2, shift) for shift in near])
    far_downs_out = pull_slices(weights, [(2, shift) for shift in far])
    (tokens,), near_gates_out, far_gates_out = joined((tokens,), near_gates_out, far_gates_out)
    (tokens,), near_gates_out = joined((tokens,), near_gates_out)
    near_gates = shift_blocks(near_gates_out, near)

    def dispatch(sent):
        return ep_exchange(sent.reshape(ep_count, capacity, -1)).reshape(slots, -1)

    (tokens,), = joined((tokens,))
    (tokens,), = joined((tokens,))
    cos, sin = rope_tables(doc_ids, head_dim)
    (
        first_normed, rate_first, heads_low, query_raw, query_low, probs, key_raw, key_low, value_low,
    ) = attend(
        tokens, doc_ids, query_weight, key_matrix, value_matrix, attn_gain, query_gain, key_gain, cos, sin
    )

    (cotangent, heads_low), = joined((cotangent, heads_low))
    (cotangent,), near_gates = joined((cotangent,), near_gates)
    (cotangent,), far_gates_out = joined((cotangent,), far_gates_out)
    far_gates = shift_blocks(far_gates_out, far)
    send_mask, turned_mask, routed, sent_grads = route(
        routes, cotangent, total_experts, capacity, ep_count, tp_count
    )
    (heads_low, sent_grads), = joined((heads_low, sent_grads))
    (sent_grads,), = joined((sent_grads,))
    (sent_grads,), = joined((sent_grads,))
    (heads_low,), far_gates = joined((heads_low,), far_gates)
    (heads_low,), = joined((heads_low,))
    attn_parts = project(heads_low, [output_weight], weight=PROJECT_FIRST)
    grads_in = dispatch(sent_grads)

    tokens_own = row_block(tokens, tp_index, tp_count).astype(F32)
    upstream_own = row_block(cotangent, tp_index, tp_count).astype(F32)
    hidden = tokens_own + tp_sum_blocks(attn_parts)
    rate_second = norm_rate(hidden)
    normed_own = (hidden * rate_second * mlp_gain).astype(BF)
    own = pull_slices(weights, [(0, 0), (1, 0), (2, 0)])
    (normed_own,), near_ups_out, far_ups_out, near_downs_out, far_downs_out = joined((normed_own,), near_ups_out, far_ups_out, near_downs_out, far_downs_out)
    (normed_own,), = joined((normed_own,))
    (normed_own,), near_ups_out, far_ups_out, near_downs_out = joined((normed_own,), near_ups_out, far_ups_out, near_downs_out)
    near_ups = shift_blocks(near_ups_out, near)
    far_ups = shift_blocks(far_ups_out, far)
    near_downs = shift_blocks(near_downs_out, near)
    normed_blocks = tp_spread(normed_own)
    normed_blocks, far_downs_out = joined(normed_blocks, far_downs_out)
    far_downs = shift_blocks(far_downs_out, far)
    normed_blocks, = joined(normed_blocks)
    sent_rows, normed_second = fill(normed_blocks, turned_mask)
    rows_in = dispatch(sent_rows)
    (normed_second,), far_downs = joined((normed_second,), far_downs)

    columns = jnp.arange(total_experts, dtype=jnp.int32)
    slot_logits = jnp.dot(rows_in, router_weight, preferred_element_type=F32)
    slot_logits = jnp.where(grads_in[:, width:].astype(F32) > 0.5, slot_logits, MASKED)
    slot_exp = jnp.exp(slot_logits - jnp.max(slot_logits, axis=-1, keepdims=True))
    own_expert = (columns == ep_index * tp_count + tp_index).astype(F32)
    probs_in = jnp.sum(slot_exp * own_expert[None, :], axis=-1) / jnp.sum(slot_exp, axis=-1)

    (grads_in,), near_downs = joined((grads_in,), near_downs)
    downs = [own[2], near_downs[0], *far_downs, near_downs[1]]
    down_full = jnp.concatenate(downs, axis=0)
    act_grad = hidden_grads(grads_in, downs)
    (act_grad,), near_ups, far_ups = joined((act_grad,), near_ups, far_ups)
    gates = [own[0], near_gates[0], *far_gates, near_gates[1]]
    ups = [own[1], near_ups[0], *far_ups, near_ups[1]]
    rows_grad, act_low, gate_back, up_back = expert_pass(rows_in, act_grad, gates, ups, total_experts)
    (normed_second, act_low), = joined((normed_second, act_low))
    gate_probs, weigh_back = gate_weights(
        normed_second, router_weight, routed, send_mask, capacity, ep_count, tp_count
    )
    back_rows = dispatch(rows_grad)
    expert_out = jnp.dot(act_low, down_full, preferred_element_type=F32).astype(BF)

    def expert_grad(left, right):
        weighed = (left.astype(F32) * probs_in[:, None]).astype(BF)
        return lax.dot_general(weighed, right, ROWS, preferred_element_type=F32).astype(BF)

    down_blocks = push_blocks(expert_grad(act_low, grads_in[:, :width]))
    gate_part = expert_grad(gate_back, rows_in)
    up_part = expert_grad(up_back, rows_in)
    unit = gate_part.shape[0] // tp_count

    def part_of(part, shift):
        return part[shift * unit : (shift + 1) * unit]

    own_parts = [part_of(gate_part, 0), part_of(up_part, 0)]
    gate_near = [part_of(gate_part, shift) for shift in near]
    up_near = [part_of(up_part, shift) for shift in near]
    far_parts = [
        jnp.concatenate([part_of(gate_part, shift), part_of(up_part, shift)], axis=0) for shift in far
    ]
    back_near, back_far = [-shift for shift in near], [-shift for shift in far]
    down_group = list(down_blocks)
    pushed_gates = shift_blocks(gate_near, back_near)
    held = (back_rows, expert_out, *down_group)
    held, pushed_gates, own_parts, up_near, far_parts = joined(held, pushed_gates, own_parts, up_near, far_parts)
    back_rows, expert_out, *down_group = held

    input_parts = combine(weigh_back, send_mask, back_rows, width, capacity)
    down_group, input_parts = joined(down_group, input_parts)
    down_wgrad = place_experts(down_group)
    expert_out, *input_parts = joined((expert_out, *input_parts))[0]
    returned = [dispatch(expert_out)]
    back_sum = tp_sum_blocks(input_parts)

    gate_grad = back_sum[:, width:]
    probs_own = row_block(gate_probs, tp_index, tp_count)
    gate_mean = jnp.sum(probs_own * gate_grad, axis=-1, keepdims=True)
    logit_own = (probs_own * (gate_grad - gate_mean)).astype(BF)
    router_input = lax.dot_general(logit_own, router_weight, COLS, preferred_element_type=F32)
    second_grad = router_input + back_sum[:, :width]
    mlp_gain_part = jnp.sum(second_grad * hidden * rate_second, axis=0)
    hidden_grad = upstream_own + norm_back(hidden, rate_second, mlp_gain, second_grad)
    branch_blocks = tp_spread(jnp.concatenate([hidden_grad.astype(BF), logit_own], axis=1))
    branch_blocks, up_near = joined(branch_blocks, up_near)
    pushed_ups = shift_blocks(up_near, back_near)
    branch_blocks, = joined(branch_blocks)

    branch_low, logit_grad, raw_grads, head_gains = attend_back(
        branch_blocks, output_weight, query_raw, query_low, probs, key_raw, key_low, value_low, cos, sin, query_gain, key_gain
    )
    (branch_low, raw_grads), = joined((branch_low, raw_grads))
    (raw_grads,), pushed_ups = joined((raw_grads,), pushed_ups)
    attn_gain_part, *first_parts = project(
        raw_grads, [query_weight, key_matrix, value_matrix], tokens, rate_first, weight=PROJECT_LAST
    )
    share = width // ep_count
    gains = jnp.concatenate(
        [
            attn_gain_part.reshape(ep_count, share),
            mlp_gain_part.reshape(ep_count, share),
            jnp.broadcast_to(head_gains[:2].reshape(1, -1), (ep_count, 2 * head_dim)),
        ],
        axis=1,
    )
    raw_keep, raw_send = grad_halves([(first_normed, raw_grads)], weight=HALVES_FIRST)
    raw_got = swap_cores(raw_send)
    extra = core_sum(gains)
    first_grad = tp_sum_blocks(first_parts)
    (first_grad,), returned = joined((first_grad,), returned)
    (first_grad, branch_low), = joined((first_grad, branch_low))
    (branch_low,), = joined((branch_low,))
    logits_wide = jnp.pad(logit_grad, ((0, 0), (0, -total_experts % 128)))
    later_pair = grad_halves([(branch_low, heads_low), (normed_second, logits_wide)], weight=HALVES_LATER)
    later_pair = (later_pair[0], swap_cores(later_pair[1]))
    (first_grad,), far_parts = joined((first_grad,), far_parts)
    pushed_far = shift_blocks(far_parts, back_far)
    sums = pair_sums([(raw_keep, raw_got), later_pair], extra)
    rate_own = row_block(rate_first, tp_index, tp_count)[:, :1]
    (first_grad, sums), = joined((first_grad, sums))
    tokens_own_grad = hidden_grad + norm_back(tokens_own, rate_own, attn_gain, first_grad)
    token_blocks = tp_spread(tokens_own_grad.astype(BF))
    token_blocks, = joined(token_blocks)
    tokens_grad = tp_join(token_blocks)

    returned, = joined(returned)
    layer_own = (hidden + tp_sum_blocks(mix(weigh_back, returned[0]))).astype(BF)
    (layer_own,), = joined((layer_own,))

    widths = (
        query_weight.shape[1], key_matrix.shape[1], value_matrix.shape[1], heads_low.shape[1], total_experts + -total_experts % 128,
    )
    query_wgrad, key_wgrad, value_wgrad, output_wgrad, router_wgrad, gain_rows = chip_sums(
        chip_exchange(sums), widths, share
    )
    many = gains.shape[1] // 128
    gain_total = tp_sum((gain_rows[:many] + gain_rows[many : 2 * many]).reshape(-1))
    layer_blocks = tp_spread(layer_own)
    gate_blocks = [own_parts[0], pushed_gates[0], *[block[:unit] for block in pushed_far], pushed_gates[1]]
    up_blocks = [own_parts[1], pushed_ups[0], *[block[unit:] for block in pushed_far], pushed_ups[1]]
    layer_out = tp_join(layer_blocks)
    attn_gain_grad, mlp_gain_grad = gain_total[:share], gain_total[share : 2 * share]
    query_gain_grad = gain_total[2 * share : 2 * share + head_dim]
    key_gain_grad = gain_total[2 * share + head_dim :]
    return (
        layer_out,
        tokens_grad,
        query_wgrad,
        key_wgrad,
        value_wgrad,
        output_wgrad,
        attn_gain_grad,
        query_gain_grad,
        key_gain_grad,
        mlp_gain_grad,
        router_wgrad[:, :total_experts],
        jnp.swapaxes(place_experts(gate_blocks), 1, 2),
        jnp.swapaxes(place_experts(up_blocks), 1, 2),
        down_wgrad,
    )


def solution(mesh):
    in_specs = (
        P("ep", None),
        P("ep"),
        P("ep", None),
        P(None, "tp"),
        P(None, "tp"),
        P(None, "tp"),
        P(None, "tp"),
        P(),
        P(),
        P(),
        P(),
        P(),
        P("ep", None, "tp"),
        P("ep", None, "tp"),
        P("ep", "tp", None),
        P("ep", None),
    )
    out_specs = (
        P("ep", None),
        P("ep", None),
        P("ep", "tp"),
        P("ep", "tp"),
        P("ep", "tp"),
        P("ep", "tp"),
        P("ep"),
        P(),
        P(),
        P("ep"),
        P("ep", None),
        P("ep", None, "tp"),
        P("ep", None, "tp"),
        P("ep", "tp", None),
    )
    return jax.shard_map(
        per_device, mesh=mesh, in_specs=in_specs, out_specs=out_specs, check_vma=False
    )
```
